256 devices in a mesh: rep: 8 (over z_lo, x), shard: 32 (over z_hi, y, core).
Axes of the slice: x: 4, y: 4, z: 8 (z_hi: 4, z_lo: 2; z = z_hi * 2 + z_lo), core: 2. Of those that a mesh axis runs over, the one named last changes fastest.
Arguments:
- images: bfloat16 [512, 16, 16, 1024], P(('rep', 'shard')), may hold values from -6 to 6
- kernel: bfloat16 [9216, 512], P('shard'), may hold values from -0.0625 to 0.0625
- gn_gain: float32 [1024], replicated, may hold values from 0.1 to 1.9
- gn_bias: float32 [1024], replicated, may hold values from -3 to 3
- conv_bias: float32 [512], replicated, may hold values from -3 to 3
- cotangent: bfloat16 [512, 8, 8, 512], P(('rep', 'shard')), may hold values from -6 to 6
Outputs:
- outputs: bfloat16 [512, 8, 8, 512], P(('rep', 'shard'))
- input_grad: bfloat16 [512, 16, 16, 1024], P(('rep', 'shard'))
- kernel_grad: float32 [9216, 512], P('shard')
- bias_grad: float32 [512], replicated
The draws below stay inside these ranges and needn't reach their ends.
All inputs are finite; a program needn't handle non-finite values.
Results may differ from the reference program's by a relative error of at most 0.0041.
Values may be sent and summed in bfloat16 or wider, within the bound.
No kernel may reach another device: no remote copies, remote signals or barrier semaphores. Data moves between devices by JAX's collectives and lax.ppermute only.
A program may use at most 128 MiB of HBM per device.

```python
import jax
import jax.numpy as jnp
from jax import lax

CIN = 1024
COUT = 512
GROUPS = 32
HIN = 16
HOUT = 8
IMAGES = 512


def levels(key, shape, shards, low, top_value):
    loudness, own = 1.0, jax.random.fold_in(key, 6)
    for position, blocks in shards:
        steps = jnp.exp(jax.random.uniform(jax.random.fold_in(own, position), (blocks,), jnp.float32, low / len(shards), top_value / len(shards)))
        loudness = loudness * jnp.repeat(steps, shape[position] // blocks).reshape([-1 if axis == position else 1 for axis in range(len(shape))])
    return loudness


def gaussian(stream_key, extent, width, most, shards=(), held_as=jnp.bfloat16):
    array = jax.random.normal(stream_key, extent, jnp.float32) * width
    if len(shards) > 0:
        array = levels(stream_key, extent, shards, -0.22, 0.18) * array
    return jnp.clip(array, min=-most, max=most).astype(held_as)


def setup_inputs(seed: int = 0) -> dict:
    key_list = jax.random.split(jax.random.key(seed), 7)
    images = gaussian(key_list[0], (IMAGES, HIN, HIN, CIN), 1.0, 6.0, ((0, 256),))
    kernel = gaussian(key_list[1], (9 * CIN, COUT), (9 * CIN) ** -0.5, 0.0625, ((0, 32),))
    gn_gain = jnp.clip(1.0 + 0.18 * jax.random.normal(key_list[2], (CIN,), jnp.float32), 0.1, 1.9)
    gn_bias = gaussian(key_list[3], (CIN,), 0.5, 3.0, (), jnp.float32)
    conv_bias = gaussian(key_list[4], (COUT,), 0.5, 3.0, (), jnp.float32)
    cotangent = gaussian(key_list[5], (IMAGES, HOUT, HOUT, COUT), 1.0, 6.0, ((0, 256),))
    return dict(images=images, kernel=kernel, gn_gain=gn_gain, gn_bias=gn_bias, conv_bias=conv_bias, cotangent=cotangent)


def norm_act(values, gain, shift):
    batch, rows, cols, chans = values.shape
    grouped = values.reshape(batch, rows, cols, GROUPS, chans // GROUPS)
    center = lax.optimization_barrier(jnp.mean(grouped, axis=(1, 2, 4), keepdims=True))
    spread = lax.optimization_barrier(jnp.mean(jnp.square(grouped - center), axis=(1, 2, 4), keepdims=True))
    normed = ((grouped - center) * lax.rsqrt(spread + 1e-05)).reshape(batch, rows, cols, chans)
    return jax.nn.silu(normed * gain + shift)

def make_patches(act):
    batch, rows, cols, chans = act.shape
    padded = jnp.pad(act, ((0, 0), (1, 1), (1, 1), (0, 0)))
    taps = []
    for ky in range(3):
        for kx in range(3):
            taps.append(padded[:, ky:ky + rows:2, kx:kx + cols:2, :])
    stacked = jnp.concatenate(taps, axis=3)
    return stacked.reshape(batch * (rows // 2) * (cols // 2), 9 * chans)

def fold_patches(dcols, batch, rows, cols, chans):
    parts = dcols.reshape(batch, rows // 2, cols // 2, 9, chans)
    total = jnp.zeros((batch, rows + 2, cols + 2, chans), jnp.float32)
    zero = jnp.zeros((), jnp.float32)
    for ky in range(3):
        for kx in range(3):
            piece = parts[:, :, :, 3 * ky + kx, :]
            total = total + lax.pad(piece, zero, ((0, 0, 0), (ky, 3 - ky, 1), (kx, 3 - kx, 1), (0, 0, 0)))
    return total[:, 1:rows + 1, 1:cols + 1, :]

def reference(images, kernel, gn_gain, gn_bias, conv_bias, cotangent):

    def one_image(carry, inputs):
        image, cot = inputs
        act, pull = jax.vjp(lambda v: norm_act(v, gn_gain, gn_bias), image[None].astype(jnp.float32))
        columns = make_patches(act.astype(jnp.bfloat16))
        result = (jnp.dot(columns, kernel, preferred_element_type=jnp.float32) + conv_bias).astype(jnp.bfloat16)
        grad_out = cot.reshape(-1, COUT)
        dcols = lax.dot_general(grad_out, kernel, (((1,), (1,)), ((), ())), preferred_element_type=jnp.float32)
        dact = fold_patches(dcols, 1, HIN, HIN, CIN)
        back = pull(dact)[0].astype(jnp.bfloat16)
        wsum = carry[0] + lax.dot_general(columns, grad_out, (((0,), (0,)), ((), ())), preferred_element_type=jnp.float32)
        bsum = carry[1] + lax.optimization_barrier(jnp.sum(grad_out.astype(jnp.float32), axis=0))
        return ((wsum, bsum), (result.reshape(HOUT, HOUT, COUT), back[0]))
    start = (jnp.zeros((9 * CIN, COUT), jnp.float32), jnp.zeros((COUT,), jnp.float32))
    (wsum, bsum), (outputs, input_grad) = lax.scan(one_image, start, (images, cotangent))
    return (outputs, input_grad, wsum / IMAGES, bsum / IMAGES)
```

```python
import functools

import jax
import jax.numpy as jnp
from jax import lax
from jax.experimental import pallas as pl
from jax.experimental.pallas import tpu as pltpu
from jax.sharding import PartitionSpec as P

BF = jnp.bfloat16
F32 = jnp.float32
AXES = ("rep", "shard")
CIN, COUT, HALF = 1024, 512, 256
GSIZE = 32
IMAGES = 512
EPS = 1e-05
VMEM_MB = 56 * 1024 * 1024
CHUNK, PER_CHIP, NA, NB, QA, QB = 16, 36, 16, 20, 4, 5
TAPS = [(ky, kx) for ky in range(3) for kx in range(3)]


def source(k):
    return (0, 0) if k == 1 else (1, 1 if k == 0 else 0)


def position():
    rep, shard = lax.axis_index("rep"), lax.axis_index("shard")
    return lax.rem(rep, 4), lax.rem(shard // 2, 4), shard // 8, lax.rem(shard, 2)


def number(x, y, z, core):
    return ((z % 2) * 4 + x) * 32 + ((z // 2) * 4 + y) * 2 + core


@functools.lru_cache(maxsize=None)
def pairs(dx, dy, dz, swap):
    out = []
    for x in range(4):
        for y in range(4):
            for z in range(8):
                for core in range(2):
                    src = number((x + dx) % 4, (y + dy) % 4, (z + dz) % 8, core ^ swap)
                    out.append((src, number(x, y, z, core)))
    return sorted(out)


def fetch(value, dx=0, dy=0, dz=0, swap=0):
    return lax.ppermute(value, AXES, pairs(dx, dy, dz, swap))


def pair_low(value):
    out = []
    for x in range(4):
        for y in range(4):
            for z in range(8):
                for core in range(2):
                    out.append((number(x, y, z ^ 1, core), number(x, y, z, core)))
    return lax.ppermute(value, AXES, sorted(out))


def turn(index, step):
    return lax.rem(index + step, 4)


def call(body, outs, args, flops=0, moved=None, scratch=(), specs=None, out_specs=None, grid=None, **kw):
    if moved is None:
        moved = sum(a.size * a.dtype.itemsize for a in args) + sum(
            o.size * o.dtype.itemsize for o in outs
        )
    params = dict(kw)
    if grid is not None:
        params["grid"] = grid
    if specs is not None:
        params["in_specs"] = specs
    if out_specs is not None:
        params["out_specs"] = out_specs
    return pl.pallas_call(
        body,
        out_shape=outs,
        scratch_shapes=list(scratch),
        compiler_params=pltpu.CompilerParams(vmem_limit_bytes=VMEM_MB),
        cost_estimate=pl.CostEstimate(flops=flops, bytes_accessed=moved, transcendentals=0),
        **params,
    )(*args)


def arr(shape, dtype):
    return jax.ShapeDtypeStruct(shape, dtype)


def group_mean(rows):
    a = lax.broadcasted_iota(jnp.int32, (128, 128), 0) // GSIZE
    b = lax.broadcasted_iota(jnp.int32, (128, 128), 1) // GSIZE
    ones = jnp.where(a == b, 1.0, 0.0).astype(F32)
    total = lax.dot_general(
        rows,
        ones,
        (((1,), (0,)), ((), ())),
        precision=lax.Precision.HIGHEST,
        preferred_element_type=F32,
    )
    return total * (1.0 / (256 * GSIZE))


def stack_rows(a, b):
    row = lax.broadcasted_iota(jnp.int32, (8, 128), 0)
    return jnp.where(row == 0, a, jnp.where(row == 1, b, 0.0))


def norm_body(x_ref, gain_ref, bias_ref, act_ref, plane_ref, stat_ref, buf):
    x = x_ref[...].astype(F32).reshape(2, 256, 128)
    sums = [jnp.sum(x[i], axis=0, keepdims=True) for i in range(2)]
    mean = group_mean(stack_rows(*sums))
    sq = [jnp.sum(jnp.square(x[i] - mean[i : i + 1]), axis=0, keepdims=True) for i in range(2)]
    rstd = lax.rsqrt(group_mean(stack_rows(*sq)) + EPS)
    stat_ref[0] = mean
    stat_ref[1] = rstd
    buf[...] = x.reshape(512, 128)
    gain, bias = gain_ref[...], bias_ref[...]
    for pj in range(2):
        part = buf[pl.ds(pj, 256, stride=2), :].reshape(2, 8, 2, 64 // 8, 128)
        for pi in range(2):
            for i in range(2):
                xp = part[i, :, pi].reshape(64, 128)
                y = (xp - mean[i : i + 1]) * rstd[i : i + 1] * gain + bias
                rows = slice(64 * i, 64 * i + 64)
                act_ref[2 * pi + pj, rows, :] = (y * jax.nn.sigmoid(y)).astype(BF)
                plane_ref[2 * pi + pj, rows, :] = xp.astype(BF)


def norm_forward(images, gain, bias):
    plane = arr((4, 128, CIN), BF)
    vec = pl.BlockSpec((1, 128), lambda c: (0, c))
    block = pl.BlockSpec((4, 128, 128), lambda c: (0, 0, c))
    return call(
        norm_body,
        (plane, plane, arr((2, 8, CIN), F32)),
        (images, gain.reshape(1, CIN), bias.reshape(1, CIN)),
        flops=20 * images.size,
        scratch=(pltpu.VMEM((512, 128), F32),),
        grid=(CIN // 128,),
        specs=[pl.BlockSpec((2, 16, 16, 128), lambda c: (0, 0, 0, c)), vec, vec],
        out_specs=(block, block, pl.BlockSpec((2, 8, 128), lambda c: (0, 0, c))),
    )


def norm_back_body(xp_ref, own_ref, got_ref, gain_ref, bias_ref, stat_ref, out_ref, buf):
    gain, bias = gain_ref[...], bias_ref[...]
    mean, rstd = stat_ref[0], stat_ref[1]
    hats, grads, one, two = [], [], [], []
    for i in range(2):
        rows = slice(64 * i, 64 * i + 64)
        m, r = mean[i : i + 1], rstd[i : i + 1]
        h_list, g_list, s1, s2 = [], [], 0.0, 0.0
        for p in range(4):
            hat = (xp_ref[p, rows, :].astype(F32) - m) * r
            y = hat * gain + bias
            s = jax.nn.sigmoid(y)
            d = own_ref[p, rows, :] + got_ref[p, rows, :]
            g = d * (s * (1.0 + y * (1.0 - s))) * gain
            s1 = s1 + jnp.sum(g, axis=0, keepdims=True)
            s2 = s2 + jnp.sum(g * hat, axis=0, keepdims=True)
            h_list.append(hat)
            g_list.append(g)
        hats.append(h_list)
        grads.append(g_list)
        one.append(s1)
        two.append(s2)
    mean1 = group_mean(stack_rows(*one))
    mean2 = group_mean(stack_rows(*two))
    for pj in range(2):
        parts = []
        for i in range(2):
            both = []
            for pi in range(2):
                p = 2 * pi + pj
                dx = rstd[i : i + 1] * (
                    grads[i][p] - mean1[i : i + 1] - hats[i][p] * mean2[i : i + 1]
                )
                both.append(dx.reshape(8, 1, 8, 128))
            parts.append(jnp.concatenate(both, axis=1).reshape(128, 128))
        buf[pl.ds(pj, 256, stride=2), :] = jnp.concatenate(parts, axis=0)
    out_ref[...] = buf[...].astype(BF).reshape(2, 16, 16, 128)


def norm_backward(planes, own, got, gain, bias, stat):
    vec = pl.BlockSpec((1, 128), lambda c: (0, c))
    block = pl.BlockSpec((4, 128, 128), lambda c: (0, 0, c))
    return call(
        norm_back_body,
        (arr((2, 16, 16, CIN), BF),),
        (planes, own, got, gain.reshape(1, CIN), bias.reshape(1, CIN), stat),
        flops=40 * planes.size,
        scratch=(pltpu.VMEM((512, 128), F32),),
        grid=(CIN // 128,),
        specs=[block, block, block, vec, vec, pl.BlockSpec((2, 8, 128), lambda c: (0, 0, c))],
        out_specs=(pl.BlockSpec((2, 16, 16, 128), lambda c: (0, 0, 0, c)),),
    )[0]


def shifted(cot, si, sj):
    row = lax.broadcasted_iota(jnp.int32, cot.shape, 0)
    value = cot
    if sj:
        value = jnp.where(row % 8 == 7, 0.0, pltpu.roll(value, cot.shape[0] - 1, 0))
    if si:
        value = jnp.where((row // 8) % 8 == 7, 0.0, pltpu.roll(value, cot.shape[0] - 8, 0))
    return value


def delayed(acc, si, sj):
    row = lax.broadcasted_iota(jnp.int32, acc.shape, 0)
    value = acc
    if sj:
        value = jnp.where(row % 8 == 0, 0.0, pltpu.roll(value, 1, 0))
    if si:
        value = jnp.where((row // 8) % 8 == 0, 0.0, pltpu.roll(value, 8, 0))
    return value


def cot_rows(own_ref, got_ref):
    return jnp.concatenate([own_ref[...], got_ref[...]], axis=0).astype(F32)


def wgrad_body(act_own, act_got, cot_own, cot_got, *refs):
    outs_a, outs_b = refs[:4], refs[4:8]
    whole, tail, sem = refs[8], refs[9], refs[10]
    x, y, _, _ = position()
    cot = cot_rows(cot_own, cot_got)
    moved = {(si, sj): shifted(cot, si, sj).astype(BF) for si in range(2) for sj in range(2)}
    for t, (ky, kx) in enumerate(TAPS):
        (pi, si), (pj, sj) = source(ky), source(kx)
        act = jnp.concatenate([act_own[2 * pi + pj], act_got[2 * pi + pj]], axis=0)
        grad = lax.dot_general(
            act, moved[si, sj], (((0,), (0,)), ((), ())), preferred_element_type=F32
        ).astype(BF)
        for q in range(16):
            n = t * 64 + 4 * q
            r, k = n // PER_CHIP, n % PER_CHIP
            whole[r // 4, r % 4, k : k + 4] = grad[64 * q : 64 * q + 64].reshape(4, CHUNK, HALF)
    bias = jnp.sum(cot, axis=0, keepdims=True)
    high = bias.astype(BF).astype(F32)
    low = bias - high
    row = lax.broadcasted_iota(jnp.int32, (CHUNK, HALF), 0)
    tail[0] = jnp.where(row == 0, high, jnp.where(row == 1, low, 0.0)).astype(BF)
    copies = []
    for d in range(4):
        there = turn(x, d)
        copies.append(
            pltpu.make_async_copy(
                whole.at[:, :, pl.ds(QA * there, QA)], outs_a[d], sem.at[len(copies)]
            )
        )
        there = turn(y, d)
        for z in range(4):
            copies.append(
                pltpu.make_async_copy(
                    whole.at[z, there, pl.ds(NA, NB)],
                    outs_b[d].at[pl.ds(NB * z, NB)],
                    sem.at[len(copies)],
                )
            )
        copies.append(
            pltpu.make_async_copy(tail, outs_b[d].at[pl.ds(4 * NB, 1)], sem.at[len(copies)])
        )
    for copy in copies:
        copy.start()
    for copy in copies:
        copy.wait()


def wgrad(act_own, act_got, cot_own, cot_got):
    vm = pl.BlockSpec(memory_space=pltpu.VMEM)
    hbm = pl.BlockSpec(memory_space=pl.ANY)
    outs = (arr((4, 4, QA, CHUNK, HALF), BF),) * 4 + (arr((4 * NB + 1, CHUNK, HALF), BF),) * 4
    res = call(
        wgrad_body,
        outs,
        (act_own, act_got, cot_own, cot_got),
        flops=2 * 256 * 9216 * HALF,
        scratch=(
            pltpu.VMEM((4, 4, PER_CHIP, CHUNK, HALF), BF),
            pltpu.VMEM((1, CHUNK, HALF), BF),
            pltpu.SemaphoreType.DMA((24,)),
        ),
        specs=[vm] * 4,
        out_specs=(hbm,) * 8,
    )
    return res[:4], res[4:]


def conv_body(*refs):
    ka, kb = refs[:4], refs[4:8]
    act_own, act_got, cot_own, cot_got, cbias = refs[8:13]
    out_own, out_other, dact_own, dact_other = refs[13:17]
    whole, sem = refs[17], refs[18]
    x, y, _, _ = position()
    copies = []
    for d in range(4):
        copies.append(
            pltpu.make_async_copy(
                ka[d], whole.at[:, :, pl.ds(QA * turn(x, d), QA)], sem.at[2 * d]
            )
        )
        copies.append(
            pltpu.make_async_copy(
                kb[d], whole.at[:, turn(y, d), pl.ds(NA, NB)], sem.at[2 * d + 1]
            )
        )
    for copy in copies:
        copy.start()
    cot = cot_rows(cot_own, cot_got)
    moved = {(si, sj): shifted(cot, si, sj).astype(BF) for si in range(2) for sj in range(2)}
    for copy in copies:
        copy.wait()

    def tap(t):
        parts = []
        for q in range(16):
            n = t * 64 + 4 * q
            r, k = n // PER_CHIP, n % PER_CHIP
            parts.append(whole[r // 4, r % 4, k : k + 4].reshape(64, HALF))
        return jnp.concatenate(parts, axis=0)

    total = None
    for si in range(2):
        for sj in range(2):
            acc = None
            for t, (ky, kx) in enumerate(TAPS):
                (pi, a), (pj, b) = source(ky), source(kx)
                if (a, b) != (si, sj):
                    continue
                act = jnp.concatenate([act_own[2 * pi + pj], act_got[2 * pi + pj]], axis=0)
                term = jnp.dot(act, tap(t), preferred_element_type=F32)
                acc = term if acc is None else acc + term
            acc = delayed(acc, si, sj)
            total = acc if total is None else total + acc
    result = (total + cbias[...]).astype(BF)
    out_own[...] = result[:128]
    out_other[...] = result[128:]
    for pi in range(2):
        for pj in range(2):
            acc = None
            for t, (ky, kx) in enumerate(TAPS):
                (a, si), (b, sj) = source(ky), source(kx)
                if (a, b) != (pi, pj):
                    continue
                term = lax.dot_general(
                    moved[si, sj], tap(t), (((1,), (1,)), ((), ())), preferred_element_type=F32
                )
                acc = term if acc is None else acc + term
            dact_own[2 * pi + pj] = acc[:128]
            dact_other[2 * pi + pj] = acc[128:]


def conv(ka, kb, act_own, act_got, cot_own, cot_got, cbias):
    vm = pl.BlockSpec(memory_space=pltpu.VMEM)
    hbm = pl.BlockSpec(memory_space=pl.ANY)
    out, dact = arr((128, HALF), BF), arr((4, 128, CIN), F32)
    return call(
        conv_body,
        (out, out, dact, dact),
        (*ka, *kb, act_own, act_got, cot_own, cot_got, cbias),
        flops=4 * 256 * 9216 * HALF,
        scratch=(
            pltpu.VMEM((4, 4, PER_CHIP, CHUNK, HALF), BF),
            pltpu.SemaphoreType.DMA((8,)),
        ),
        specs=[hbm] * 8 + [vm] * 5,
        out_specs=(vm,) * 4,
    )


def spread_z_body(a0, a1, a2, a3, a_ref, b_ref):
    _, _, z, _ = position()
    for d, ref in enumerate((a0, a1, a2, a3)):
        there = turn(z, d)
        a_ref[there] = ref[:QA]
        b_ref[there] = ref[QA:]


def spread_xy_body(a0, a1, a2, a3, b0, b1, b2, b3, a_ref, b_ref):
    x, y, _, _ = position()
    for d, (a, b) in enumerate(((a0, b0), (a1, b1), (a2, b2), (a3, b3))):
        there = turn(y, d)
        for z in range(4):
            a_ref[z, there] = a[z]
        there = turn(x, d)
        for z in range(4):
            b_ref[z, pl.ds(QB * there, QB)] = b[z]


def gather_kernel(kernel, core):
    halves = kernel.reshape(18, CHUNK, COUT)
    left, right = halves[:, :, :HALF], halves[:, :, HALF:]
    mine = jnp.where(core == 0, left, right)
    theirs = fetch(jnp.where(core == 0, right, left), swap=1)
    block = jnp.concatenate(
        [jnp.where(core == 0, mine, theirs), jnp.where(core == 0, theirs, mine)], axis=0
    )
    x = position()[0]
    piece = jnp.concatenate(
        [
            lax.dynamic_slice_in_dim(block, QA * x, QA, 0),
            lax.dynamic_slice_in_dim(block, NA + QB * x, QB, 0),
        ],
        axis=0,
    )
    got = [piece] + [fetch(piece, dz=2 * d) for d in range(1, 4)]
    a, b = call(
        spread_z_body, (arr((4, QA, CHUNK, HALF), BF), arr((4, QB, CHUNK, HALF), BF)), got
    )
    got_a = [a] + [fetch(a, dy=d) for d in range(1, 4)]
    got_b = [b] + [fetch(b, dx=d) for d in range(1, 4)]
    a, b = call(
        spread_xy_body,
        (arr((4, 4, QA, CHUNK, HALF), BF), arr((4, NB, CHUNK, HALF), BF)),
        (*got_a, *got_b),
    )
    ka = [a] + [fetch(a, dx=d) for d in range(1, 4)]
    kb = [b] + [fetch(b, dy=d) for d in range(1, 4)]
    return ka, kb


def four(refs, index):
    v = [ref[index].astype(F32) for ref in refs]
    return (v[0] + v[2]) + (v[1] + v[3])


def bias_four(refs, index):
    v = [ref[index].astype(F32) for ref in refs]
    v = [w[0:1] + w[1:2] for w in v]
    return (v[0] + v[2]) + (v[1] + v[3])


def bias_chunk(total):
    high = total.astype(BF).astype(F32)
    row = lax.broadcasted_iota(jnp.int32, (CHUNK, HALF), 0)
    return jnp.where(row == 0, high, jnp.where(row == 1, total - high, 0.0)).astype(BF)


def sum_xy_body(*refs):
    a, b = refs[:4], refs[4:8]
    out_a, out_b = refs[8:12], refs[12:16]
    x, y, _, _ = position()
    bias = bias_chunk(bias_four(b, 4 * NB))
    for d in range(4):
        there = turn(y, d)
        for z in range(4):
            out_a[d][z] = four(a, (z, there)).astype(BF)
        there = turn(x, d)
        for z in range(4):
            out_b[d][QB * z : QB * z + QB] = four(b, pl.ds(NB * z + QB * there, QB)).astype(BF)
        out_b[d][4 * QB] = bias


def sum_yx_body(*refs):
    a, b = refs[:4], refs[4:8]
    outs = refs[8:12]
    _, _, z, _ = position()
    bias = bias_chunk(bias_four(b, 4 * QB))
    for d in range(4):
        there = turn(z, d)
        outs[d][:QA] = four(a, there).astype(BF)
        outs[d][QA : QA + QB] = four(b, pl.ds(QB * there, QB)).astype(BF)
        outs[d][QA + QB] = bias


def sum_z_body(*refs):
    ins, out = refs[:4], refs[4]
    out[: QA + QB] = four(ins, pl.ds(0, QA + QB))
    row = lax.broadcasted_iota(jnp.int32, (CHUNK, HALF), 0)
    out[QA + QB] = jnp.where(row == 0, bias_four(ins, QA + QB), 0.0)


def place_body(f0, f1, f2, f3, mine, theirs, whole):
    x, _, _, core = position()
    for d, ref in enumerate((f0, f1, f2, f3)):
        there = turn(x, d)
        whole[pl.ds(QA * there, QA)] = ref[:QA]
        whole[pl.ds(NA + QB * there, QB)] = ref[QA : QA + QB]
    mine[:18] = whole[pl.ds(18 * core, 18)]
    theirs[:18] = whole[pl.ds(18 * (1 - core), 18)]
    mine[18] = f0[QA + QB]
    theirs[18] = f0[QA + QB]


def reduce_gradient(send_a, send_b, core):
    a = [send_a[0]] + [fetch(send_a[4 - d], dx=d) for d in range(1, 4)]
    b = [send_b[0]] + [fetch(send_b[4 - d], dy=d) for d in range(1, 4)]
    res = call(
        sum_xy_body,
        (arr((4, QA, CHUNK, HALF), BF),) * 4 + (arr((4 * QB + 1, CHUNK, HALF), BF),) * 4,
        (*a, *b),
    )
    send_a, send_b = res[:4], res[4:]
    a = [send_a[0]] + [fetch(send_a[4 - d], dy=d) for d in range(1, 4)]
    b = [send_b[0]] + [fetch(send_b[4 - d], dx=d) for d in range(1, 4)]
    send = call(sum_yx_body, (arr((QA + QB + 1, CHUNK, HALF), BF),) * 4, (*a, *b))
    got = [send[0]] + [fetch(send[4 - d], dz=2 * d) for d in range(1, 4)]
    part = call(sum_z_body, (arr((QA + QB + 1, CHUNK, HALF), F32),), got)[0]
    full = (part + pair_low(part)) * (1.0 / IMAGES)
    rows = full[: QA + QB]
    every = [full] + [fetch(rows, dx=d) for d in range(1, 4)]
    mine, theirs = call(
        place_body,
        (arr((19, CHUNK, HALF), F32),) * 2,
        every,
        scratch=(pltpu.VMEM((PER_CHIP, CHUNK, HALF), F32),),
    )
    got = fetch(theirs, swap=1)
    both = jnp.where(
        core == 0, jnp.concatenate([mine, got], axis=-1), jnp.concatenate([got, mine], axis=-1)
    )
    return both[:18].reshape(288, COUT), both[18, 0]


def local(images, kernel, gn_gain, gn_bias, conv_bias, cotangent):
    core = position()[3]
    cot = cotangent.reshape(128, COUT)
    left, right = cot[:, :HALF], cot[:, HALF:]
    cot_own = jnp.where(core == 0, left, right)
    cot_got = fetch(jnp.where(core == 0, right, left), swap=1)
    ka, kb = gather_kernel(kernel, core)
    act, planes, stat = norm_forward(images, gn_gain, gn_bias)
    act_got = fetch(act, swap=1)
    send_a, send_b = wgrad(act, act_got, cot_own, cot_got)
    kernel_grad, bias_grad = reduce_gradient(send_a, send_b, core)
    cbias = jnp.where(core == 0, conv_bias[:HALF], conv_bias[HALF:]).reshape(1, HALF)
    out_own, out_other, dact_own, dact_other = conv(
        ka, kb, act, act_got, cot_own, cot_got, cbias
    )
    out_got = fetch(out_other, swap=1)
    dact_got = fetch(dact_other, swap=1)
    outputs = jnp.where(
        core == 0,
        jnp.concatenate([out_own, out_got], axis=-1),
        jnp.concatenate([out_got, out_own], axis=-1),
    ).reshape(cotangent.shape)
    input_grad = norm_backward(planes, dact_own, dact_got, gn_gain, gn_bias, stat)
    return outputs, input_grad, kernel_grad, bias_grad


def solution(mesh):
    return jax.shard_map(
        local,
        mesh=mesh,
        in_specs=(
            P(AXES, None, None, None),
            P("shard", None),
            P(),
            P(),
            P(),
            P(AXES, None, None, None),
        ),
        out_specs=(
            P(AXES, None, None, None),
            P(AXES, None, None, None),
            P("shard", None),
            P(),
        ),
        check_vma=False,
    )
```

```python
import functools

import jax
import jax.numpy as jnp
from jax import lax
from jax.experimental import pallas as pl
from jax.experimental.pallas import tpu as pltpu
from jax.sharding import PartitionSpec as P

BF = jnp.bfloat16
F32 = jnp.float32
AXES = ("rep", "shard")
CIN, COUT, HALF = 1024, 512, 256
GSIZE = 32
IMAGES = 512
EPS = 1e-05
MIB = 1024 * 1024
CHUNK, PER_CHIP, NA, NB, QA, QB = 16, 36, 16, 20, 4, 5
TAPS = [(ky, kx) for ky in range(3) for kx in range(3)]


def source(k):
    return (0, 0) if k == 1 else (1, 1 if k == 0 else 0)


def position():
    rep, shard = lax.axis_index("rep"), lax.axis_index("shard")
    return lax.rem(rep, 4), lax.rem(shard // 2, 4), shard // 8, lax.rem(shard, 2)


def number(x, y, z, core):
    return ((z % 2) * 4 + x) * 32 + ((z // 2) * 4 + y) * 2 + core


@functools.lru_cache(maxsize=None)
def pairs(dx, dy, dz, swap):
    out = []
    for x in range(4):
        for y in range(4):
            for z in range(8):
                for core in range(2):
                    src = number((x + dx) % 4, (y + dy) % 4, (z + dz) % 8, core ^ swap)
                    out.append((src, number(x, y, z, core)))
    return sorted(out)


def fetch(value, dx=0, dy=0, dz=0, swap=0):
    return lax.ppermute(value, AXES, pairs(dx, dy, dz, swap))


def pair_low(value):
    out = []
    for x in range(4):
        for y in range(4):
            for z in range(8):
                for core in range(2):
                    out.append((number(x, y, z ^ 1, core), number(x, y, z, core)))
    return lax.ppermute(value, AXES, sorted(out))


def turn(index, step):
    return lax.rem(index + step, 4)


def call(body, outs, args, flops=0, moved=None, scratch=(), specs=None, out_specs=None, grid=None, vmem=8, **kw):
    if moved is None:
        moved = sum(a.size * a.dtype.itemsize for a in args) + sum(
            o.size * o.dtype.itemsize for o in outs
        )
    params = dict(kw)
    if grid is not None:
        params["grid"] = grid
    if specs is not None:
        params["in_specs"] = specs
    if out_specs is not None:
        params["out_specs"] = out_specs
    return pl.pallas_call(
        body,
        out_shape=outs,
        scratch_shapes=list(scratch),
        compiler_params=pltpu.CompilerParams(vmem_limit_bytes=vmem * MIB),
        cost_estimate=pl.CostEstimate(flops=flops, bytes_accessed=moved, transcendentals=0),
        **params,
    )(*args)


def arr(shape, dtype):
    return jax.ShapeDtypeStruct(shape, dtype)


def group_mean(rows):
    a = lax.broadcasted_iota(jnp.int32, (128, 128), 0) // GSIZE
    b = lax.broadcasted_iota(jnp.int32, (128, 128), 1) // GSIZE
    ones = jnp.where(a == b, 1.0, 0.0).astype(F32)
    total = lax.dot_general(
        rows,
        ones,
        (((1,), (0,)), ((), ())),
        precision=lax.Precision.HIGHEST,
        preferred_element_type=F32,
    )
    return total * (1.0 / (256 * GSIZE))


def stack_rows(a, b):
    row = lax.broadcasted_iota(jnp.int32, (8, 128), 0)
    return jnp.where(row == 0, a, jnp.where(row == 1, b, 0.0))


def norm_body(x_ref, gain_ref, bias_ref, act_ref, plane_ref, stat_ref, buf):
    x = x_ref[...].astype(F32).reshape(2, 256, 128)
    sums = [jnp.sum(x[i], axis=0, keepdims=True) for i in range(2)]
    mean = group_mean(stack_rows(*sums))
    sq = [jnp.sum(jnp.square(x[i] - mean[i : i + 1]), axis=0, keepdims=True) for i in range(2)]
    rstd = lax.rsqrt(group_mean(stack_rows(*sq)) + EPS)
    stat_ref[0] = mean
    stat_ref[1] = rstd
    buf[...] = x.reshape(512, 128)
    gain, bias = gain_ref[...], bias_ref[...]
    for pj in range(2):
        part = buf[pl.ds(pj, 256, stride=2), :].reshape(2, 8, 2, 64 // 8, 128)
        for pi in range(2):
            for i in range(2):
                xp = part[i, :, pi].reshape(64, 128)
                y = (xp - mean[i : i + 1]) * rstd[i : i + 1] * gain + bias
                rows = slice(64 * i, 64 * i + 64)
                act_ref[2 * pi + pj, rows, :] = (y * jax.nn.sigmoid(y)).astype(BF)
                plane_ref[2 * pi + pj, rows, :] = xp.astype(BF)


def norm_forward(images, gain, bias):
    plane = arr((4, 128, CIN), BF)
    vec = pl.BlockSpec((1, 128), lambda c: (0, c))
    block = pl.BlockSpec((4, 128, 128), lambda c: (0, 0, c))
    return call(
        norm_body,
        (plane, plane, arr((2, 8, CIN), F32)),
        (images, gain.reshape(1, CIN), bias.reshape(1, CIN)),
        flops=20 * images.size,
        scratch=(pltpu.VMEM((512, 128), F32),),
        grid=(CIN // 128,),
        specs=[pl.BlockSpec((2, 16, 16, 128), lambda c: (0, 0, 0, c)), vec, vec],
        out_specs=(block, block, pl.BlockSpec((2, 8, 128), lambda c: (0, 0, c))),
    )


def norm_back_body(xp_ref, dact_ref, gain_ref, bias_ref, stat_ref, out_ref, buf):
    gain, bias = gain_ref[...], bias_ref[...]
    mean, rstd = stat_ref[0], stat_ref[1]
    hats, grads, one, two = [], [], [], []
    for i in range(2):
        rows = slice(64 * i, 64 * i + 64)
        m, r = mean[i : i + 1], rstd[i : i + 1]
        h_list, g_list, s1, s2 = [], [], 0.0, 0.0
        for p in range(4):
            hat = (xp_ref[p, rows, :].astype(F32) - m) * r
            y = hat * gain + bias
            s = jax.nn.sigmoid(y)
            g = dact_ref[p, rows, :] * (s * (1.0 + y * (1.0 - s))) * gain
            s1 = s1 + jnp.sum(g, axis=0, keepdims=True)
            s2 = s2 + jnp.sum(g * hat, axis=0, keepdims=True)
            h_list.append(hat)
            g_list.append(g)
        hats.append(h_list)
        grads.append(g_list)
        one.append(s1)
        two.append(s2)
    mean1 = group_mean(stack_rows(*one))
    mean2 = group_mean(stack_rows(*two))
    for pj in range(2):
        parts = []
        for i in range(2):
            both = []
            for pi in range(2):
                p = 2 * pi + pj
                dx = rstd[i : i + 1] * (
                    grads[i][p] - mean1[i : i + 1] - hats[i][p] * mean2[i : i + 1]
                )
                both.append(dx.reshape(8, 1, 8, 128))
            parts.append(jnp.concatenate(both, axis=1).reshape(128, 128))
        buf[pl.ds(pj, 256, stride=2), :] = jnp.concatenate(parts, axis=0)
    out_ref[...] = buf[...].astype(BF).reshape(2, 16, 16, 128)


def norm_backward(planes, dact, gain, bias, stat):
    vec = pl.BlockSpec((1, 128), lambda c: (0, c))
    block = pl.BlockSpec((4, 128, 128), lambda c: (0, 0, c))
    return call(
        norm_back_body,
        (arr((2, 16, 16, CIN), BF),),
        (planes, dact, gain.reshape(1, CIN), bias.reshape(1, CIN), stat),
        flops=40 * planes.size,
        scratch=(pltpu.VMEM((512, 128), F32),),
        grid=(CIN // 128,),
        specs=[block, block, vec, vec, pl.BlockSpec((2, 8, 128), lambda c: (0, 0, c))],
        out_specs=(pl.BlockSpec((2, 16, 16, 128), lambda c: (0, 0, 0, c)),),
    )[0]


def shifted(cot, si, sj):
    row = lax.broadcasted_iota(jnp.int32, cot.shape, 0)
    value = cot
    if sj:
        value = jnp.where(row % 8 == 7, 0.0, pltpu.roll(value, cot.shape[0] - 1, 0))
    if si:
        value = jnp.where((row // 8) % 8 == 7, 0.0, pltpu.roll(value, cot.shape[0] - 8, 0))
    return value


def cot_rows(own_ref, got_ref):
    return jnp.concatenate([own_ref[...], got_ref[...]], axis=0).astype(F32)


def wgrad_body(act_own, act_got, cot_own, cot_got, *refs):
    outs_a, outs_b = refs[:4], refs[4:8]
    whole, tail, sem = refs[8], refs[9], refs[10]
    x, y, _, _ = position()
    cot = cot_rows(cot_own, cot_got)
    moved = {(si, sj): shifted(cot, si, sj).astype(BF) for si in range(2) for sj in range(2)}
    for t, (ky, kx) in enumerate(TAPS):
        (pi, si), (pj, sj) = source(ky), source(kx)
        act = jnp.concatenate([act_own[2 * pi + pj], act_got[2 * pi + pj]], axis=0)
        grad = lax.dot_general(
            act, moved[si, sj], (((0,), (0,)), ((), ())), preferred_element_type=F32
        ).astype(BF)
        for q in range(16):
            n = t * 64 + 4 * q
            r, k = n // PER_CHIP, n % PER_CHIP
            whole[r // 4, r % 4, k : k + 4] = grad[64 * q : 64 * q + 64].reshape(4, CHUNK, HALF)
    bias = jnp.sum(cot, axis=0, keepdims=True)
    high = bias.astype(BF).astype(F32)
    low = bias - high
    row = lax.broadcasted_iota(jnp.int32, (CHUNK, HALF), 0)
    tail[0] = jnp.where(row == 0, high, jnp.where(row == 1, low, 0.0)).astype(BF)
    copies = []
    for d in range(4):
        there = turn(x, d)
        copies.append(
            pltpu.make_async_copy(
                whole.at[:, :, pl.ds(QA * there, QA)], outs_a[d], sem.at[len(copies)]
            )
        )
        there = turn(y, d)
        for z in range(4):
            copies.append(
                pltpu.make_async_copy(
                    whole.at[z, there, pl.ds(NA, NB)],
                    outs_b[d].at[pl.ds(NB * z, NB)],
                    sem.at[len(copies)],
                )
            )
        copies.append(
            pltpu.make_async_copy(tail, outs_b[d].at[pl.ds(4 * NB, 1)], sem.at[len(copies)])
        )
    for copy in copies:
        copy.start()
    for copy in copies:
        copy.wait()


def wgrad(act_own, act_got, cot_own, cot_got):
    vm = pl.BlockSpec(memory_space=pltpu.VMEM)
    hbm = pl.BlockSpec(memory_space=pl.ANY)
    outs = (arr((4, 4, QA, CHUNK, HALF), BF),) * 4 + (arr((4 * NB + 1, CHUNK, HALF), BF),) * 4
    res = call(
        wgrad_body,
        outs,
        (act_own, act_got, cot_own, cot_got),
        flops=2 * 256 * 9216 * HALF,
        scratch=(
            pltpu.VMEM((4, 4, PER_CHIP, CHUNK, HALF), BF),
            pltpu.VMEM((1, CHUNK, HALF), BF),
            pltpu.SemaphoreType.DMA((24,)),
        ),
        specs=[vm] * 4,
        out_specs=(hbm,) * 8,
        vmem=24,
    )
    return res[:4], res[4:]


def conv_body(k_ref, act_ref, cot_ref, bias_ref, out_ref, dact_ref, moved, total):
    t = pl.program_id(0)
    ky, kx = t // 3, lax.rem(t, 3)
    pi, pj = jnp.where(ky == 1, 0, 1), jnp.where(kx == 1, 0, 1)
    si, sj = jnp.where(ky == 0, 1, 0), jnp.where(kx == 0, 1, 0)

    @pl.when(t == 0)
    def _():
        cot = cot_ref[...].astype(F32)
        for a in range(2):
            for b in range(2):
                moved[2 * a + b] = shifted(cot, a, b).astype(BF)
        dact_ref[...] = jnp.zeros_like(dact_ref)
        total[...] = jnp.broadcast_to(bias_ref[...], total.shape)

    k = k_ref[...]
    plane = 2 * pi + pj
    term = jnp.dot(act_ref[plane], k, preferred_element_type=F32)
    row = lax.broadcasted_iota(jnp.int32, term.shape, 0)
    late = jnp.where(row % 8 == 0, 0.0, pltpu.roll(term, 1, 0))
    term = jnp.where(sj == 1, late, term)
    late = jnp.where((row // 8) % 8 == 0, 0.0, pltpu.roll(term, 8, 0))
    total[...] += jnp.where(si == 1, late, term)
    dact_ref[plane] += lax.dot_general(
        moved[2 * si + sj], k, (((1,), (1,)), ((), ())), preferred_element_type=F32
    )

    @pl.when(t == 8)
    def _():
        out_ref[...] = total[...].astype(BF)


def conv(kernel, act, cot, cbias):
    fixed = lambda *shape: pl.BlockSpec(shape, lambda t: (0,) * len(shape))
    return call(
        conv_body,
        (arr((128, COUT), BF), arr((4, 128, CIN), F32)),
        (kernel, act, cot, cbias.reshape(1, COUT)),
        flops=4 * 128 * 9216 * COUT,
        scratch=(pltpu.VMEM((4, 128, COUT), BF), pltpu.VMEM((128, COUT), F32)),
        grid=(9,),
        specs=[
            pl.BlockSpec((CIN, COUT), lambda t: (t, 0)),
            fixed(4, 128, CIN),
            fixed(128, COUT),
            fixed(1, COUT),
        ],
        out_specs=(fixed(128, COUT), fixed(4, 128, CIN)),
        vmem=52,
    )


def four(refs, index):
    v = [ref[index].astype(F32) for ref in refs]
    return (v[0] + v[2]) + (v[1] + v[3])


def bias_four(refs, index):
    v = [ref[index].astype(F32) for ref in refs]
    v = [w[0:1] + w[1:2] for w in v]
    return (v[0] + v[2]) + (v[1] + v[3])


def bias_chunk(total):
    high = total.astype(BF).astype(F32)
    row = lax.broadcasted_iota(jnp.int32, (CHUNK, HALF), 0)
    return jnp.where(row == 0, high, jnp.where(row == 1, total - high, 0.0)).astype(BF)


def sum_xy_body(*refs):
    a, b = refs[:4], refs[4:8]
    out_a, out_b = refs[8:12], refs[12:16]
    x, y, _, _ = position()
    bias = bias_chunk(bias_four(b, 4 * NB))
    for d in range(4):
        there = turn(y, d)
        for z in range(4):
            out_a[d][z] = four(a, (z, there)).astype(BF)
        there = turn(x, d)
        for z in range(4):
            out_b[d][QB * z : QB * z + QB] = four(b, pl.ds(NB * z + QB * there, QB)).astype(BF)
        out_b[d][4 * QB] = bias


def sum_yx_body(*refs):
    a, b = refs[:4], refs[4:8]
    outs = refs[8:12]
    _, _, z, _ = position()
    bias = bias_chunk(bias_four(b, 4 * QB))
    for d in range(4):
        there = turn(z, d)
        outs[d][:QA] = four(a, there).astype(BF)
        outs[d][QA : QA + QB] = four(b, pl.ds(QB * there, QB)).astype(BF)
        outs[d][QA + QB] = bias


def sum_z_body(*refs):
    ins, out = refs[:4], refs[4]
    out[: QA + QB] = four(ins, pl.ds(0, QA + QB))
    row = lax.broadcasted_iota(jnp.int32, (CHUNK, HALF), 0)
    out[QA + QB] = jnp.where(row == 0, bias_four(ins, QA + QB), 0.0)


def place_body(f0, f1, f2, f3, mine, theirs, whole):
    x, _, _, core = position()
    for d, ref in enumerate((f0, f1, f2, f3)):
        there = turn(x, d)
        whole[pl.ds(QA * there, QA)] = ref[:QA]
        whole[pl.ds(NA + QB * there, QB)] = ref[QA : QA + QB]
    mine[:18] = whole[pl.ds(18 * core, 18)]
    theirs[:18] = whole[pl.ds(18 * (1 - core), 18)]
    mine[18] = f0[QA + QB]
    theirs[18] = f0[QA + QB]


def reduce_gradient(send_a, send_b, core):
    a = [send_a[0]] + [fetch(send_a[4 - d], dx=d) for d in range(1, 4)]
    b = [send_b[0]] + [fetch(send_b[4 - d], dy=d) for d in range(1, 4)]
    res = call(
        sum_xy_body,
        (arr((4, QA, CHUNK, HALF), BF),) * 4 + (arr((4 * QB + 1, CHUNK, HALF), BF),) * 4,
        (*a, *b),
        vmem=16,
    )
    send_a, send_b = res[:4], res[4:]
    a = [send_a[0]] + [fetch(send_a[4 - d], dy=d) for d in range(1, 4)]
    b = [send_b[0]] + [fetch(send_b[4 - d], dx=d) for d in range(1, 4)]
    send = call(sum_yx_body, (arr((QA + QB + 1, CHUNK, HALF), BF),) * 4, (*a, *b))
    got = [send[0]] + [fetch(send[4 - d], dz=2 * d) for d in range(1, 4)]
    part = call(sum_z_body, (arr((QA + QB + 1, CHUNK, HALF), F32),), got)[0]
    full = (part + pair_low(part)) * (1.0 / IMAGES)
    rows = full[: QA + QB]
    every = [full] + [fetch(rows, dx=d) for d in range(1, 4)]
    mine, theirs = call(
        place_body,
        (arr((19, CHUNK, HALF), F32),) * 2,
        every,
        scratch=(pltpu.VMEM((PER_CHIP, CHUNK, HALF), F32),),
    )
    got = fetch(theirs, swap=1)
    both = jnp.where(
        core == 0, jnp.concatenate([mine, got], axis=-1), jnp.concatenate([got, mine], axis=-1)
    )
    return both[:18].reshape(288, COUT), both[18, 0]


def local(images, kernel, gn_gain, gn_bias, conv_bias, cotangent):
    core = position()[3]
    cot = cotangent.reshape(128, COUT)
    left, right = cot[:, :HALF], cot[:, HALF:]
    cot_own = jnp.where(core == 0, left, right)
    cot_got = fetch(jnp.where(core == 0, right, left), swap=1)
    full = lax.all_gather(kernel, "shard", axis=0, tiled=True)
    act, planes, stat = norm_forward(images, gn_gain, gn_bias)
    act_got = fetch(act, swap=1)
    send_a, send_b = wgrad(act, act_got, cot_own, cot_got)
    kernel_grad, bias_grad = reduce_gradient(send_a, send_b, core)
    out, dact = conv(full, act, cot, conv_bias)
    outputs = out.reshape(cotangent.shape)
    input_grad = norm_backward(planes, dact, gn_gain, gn_bias, stat)
    return outputs, input_grad, kernel_grad, bias_grad


def solution(mesh):
    return jax.shard_map(
        local,
        mesh=mesh,
        in_specs=(
            P(AXES, None, None, None),
            P("shard", None),
            P(),
            P(),
            P(),
            P(AXES, None, None, None),
        ),
        out_specs=(
            P(AXES, None, None, None),
            P(AXES, None, None, None),
            P("shard", None),
            P(),
        ),
        check_vma=False,
    )
```

```python
import functools

import jax
import jax.numpy as jnp
from jax import lax
from jax.experimental import pallas as pl
from jax.experimental.pallas import tpu as pltpu
from jax.sharding import PartitionSpec as P

BF = jnp.bfloat16
F32 = jnp.float32
AXES = ("rep", "shard")
CIN, COUT, HALF = 1024, 512, 256
GSIZE = 32
LANES = 256
IMAGES = 512
EPS = 1e-05
MIB = 1024 * 1024
CHUNK, PER_CHIP, QUARTER = 16, 36, 9
COST_NORM, COST_WGRAD, COST_CONV, COST_BACK, COST_SUM = 10**10, 2*10**10, 10**9, 10**7, 10**10
TAPS = [(ky, kx) for ky in range(3) for kx in range(3)]


def source(k):
    return (0, 0) if k == 1 else (1, 1 if k == 0 else 0)


def position():
    rep, shard = lax.axis_index("rep"), lax.axis_index("shard")
    return lax.rem(rep, 4), lax.rem(shard // 2, 4), shard // 8, lax.rem(shard, 2)


def number(x, y, z, core):
    return ((z % 2) * 4 + x) * 32 + ((z // 2) * 4 + y) * 2 + core


@functools.lru_cache(maxsize=None)
def pairs(dx, dy, dz, swap):
    out = []
    for x in range(4):
        for y in range(4):
            for z in range(8):
                for core in range(2):
                    sign = 1 - 2 * core
                    src = number(
                        (x + sign * dx) % 4, (y + sign * dy) % 4, (z + sign * dz) % 8, core ^ swap
                    )
                    out.append((src, number(x, y, z, core)))
    return sorted(out)


def fetch(value, dx=0, dy=0, dz=0, swap=0):
    with jax.named_scope(f"from_x{dx}_y{dy}_z{dz}_core{swap}"):
        return lax.ppermute(value, AXES, pairs(dx, dy, dz, swap))


def pair_low(value):
    out = []
    for x in range(4):
        for y in range(4):
            for z in range(8):
                for core in range(2):
                    out.append((number(x, y, z ^ 1, core), number(x, y, z, core)))
    with jax.named_scope("from_z_low"):
        return lax.ppermute(value, AXES, sorted(out))


def turn(index, step, core):
    return lax.rem(index + jnp.where(core == 0, step, 4 - step), 4)


def call(body, outs, args, flops=0, moved=None, scratch=(), specs=None, out_specs=None, grid=None, vmem=8, **kw):
    if moved is None:
        moved = sum(a.size * a.dtype.itemsize for a in args) + sum(
            o.size * o.dtype.itemsize for o in outs
        )
    params = dict(kw)
    if grid is not None:
        params["grid"] = grid
    if specs is not None:
        params["in_specs"] = specs
    if out_specs is not None:
        params["out_specs"] = out_specs
    return pl.pallas_call(
        body,
        out_shape=outs,
        scratch_shapes=list(scratch),
        compiler_params=pltpu.CompilerParams(vmem_limit_bytes=vmem * MIB),
        cost_estimate=pl.CostEstimate(flops=flops, bytes_accessed=moved, transcendentals=0),
        **params,
    )(*args)


def arr(shape, dtype):
    return jax.ShapeDtypeStruct(shape, dtype)


def group_mean(rows):
    a = lax.broadcasted_iota(jnp.int32, (LANES, LANES), 0) // GSIZE
    b = lax.broadcasted_iota(jnp.int32, (LANES, LANES), 1) // GSIZE
    ones = jnp.where(a == b, 1.0, 0.0).astype(F32)
    total = lax.dot_general(
        rows,
        ones,
        (((1,), (0,)), ((), ())),
        precision=lax.Precision.HIGHEST,
        preferred_element_type=F32,
    )
    return total * (1.0 / (256 * GSIZE))


def stack_rows(a, b):
    row = lax.broadcasted_iota(jnp.int32, (8, LANES), 0)
    return jnp.where(row == 0, a, jnp.where(row == 1, b, 0.0))


def norm_body(x_ref, gain_ref, bias_ref, act_ref, plane_ref, stat_ref, *bufs):
    x = x_ref[...].astype(F32).reshape(2, 256, LANES)
    sums = [jnp.sum(x[i], axis=0, keepdims=True) for i in range(2)]
    mean = group_mean(stack_rows(*sums))
    sq = [jnp.sum(jnp.square(x[i] - mean[i : i + 1]), axis=0, keepdims=True) for i in range(2)]
    rstd = lax.rsqrt(group_mean(stack_rows(*sq)) + EPS)
    stat_ref[0] = mean
    stat_ref[1] = rstd
    for h, buf in enumerate(bufs):
        buf[...] = x[:, :, 128 * h : 128 * h + 128].reshape(512, 128)
    gain, bias = gain_ref[...], bias_ref[...]
    for pj in range(2):
        part = jnp.concatenate([buf[pl.ds(pj, 256, stride=2), :] for buf in bufs], axis=-1)
        part = part.reshape(2, 8, 2, 8, LANES)
        for pi in range(2):
            for i in range(2):
                xp = part[i, :, pi].reshape(64, LANES)
                y = (xp - mean[i : i + 1]) * rstd[i : i + 1] * gain + bias
                rows = slice(64 * i, 64 * i + 64)
                act_ref[2 * pi + pj, rows, :] = (y * jax.nn.sigmoid(y)).astype(BF)
                plane_ref[2 * pi + pj, rows, :] = xp.astype(BF)


def norm_forward(images, gain, bias):
    plane = arr((4, 128, CIN), BF)
    vec = pl.BlockSpec((1, LANES), lambda c: (0, c))
    block = pl.BlockSpec((4, 128, LANES), lambda c: (0, 0, c))
    return call(
        norm_body,
        (plane, plane, arr((2, 8, CIN), F32)),
        (images, gain.reshape(1, CIN), bias.reshape(1, CIN)),
        flops=COST_NORM,
        scratch=(pltpu.VMEM((512, 128), F32),) * (LANES // 128),
        grid=(CIN // LANES,),
        specs=[pl.BlockSpec((2, 16, 16, LANES), lambda c: (0, 0, 0, c)), vec, vec],
        out_specs=(block, block, pl.BlockSpec((2, 8, LANES), lambda c: (0, 0, c))),
    )


def norm_back_body(xp_ref, own_ref, got_ref, gain_ref, bias_ref, stat_ref, out_ref, *bufs):
    gain, bias = gain_ref[...], bias_ref[...]
    mean, rstd = stat_ref[0], stat_ref[1]
    hats, grads, one, two = [], [], [], []
    for i in range(2):
        rows = slice(64 * i, 64 * i + 64)
        m, r = mean[i : i + 1], rstd[i : i + 1]
        h_list, g_list, s1, s2 = [], [], 0.0, 0.0
        for p in range(4):
            hat = (xp_ref[p, rows, :].astype(F32) - m) * r
            y = hat * gain + bias
            s = jax.nn.sigmoid(y)
            d = own_ref[p, rows, :] + got_ref[p, rows, :].astype(F32)
            g = d * (s * (1.0 + y * (1.0 - s))) * gain
            s1 = s1 + jnp.sum(g, axis=0, keepdims=True)
            s2 = s2 + jnp.sum(g * hat, axis=0, keepdims=True)
            h_list.append(hat)
            g_list.append(g)
        hats.append(h_list)
        grads.append(g_list)
        one.append(s1)
        two.append(s2)
    mean1 = group_mean(stack_rows(*one))
    mean2 = group_mean(stack_rows(*two))
    for pj in range(2):
        parts = []
        for i in range(2):
            both = []
            for pi in range(2):
                p = 2 * pi + pj
                dx = rstd[i : i + 1] * (
                    grads[i][p] - mean1[i : i + 1] - hats[i][p] * mean2[i : i + 1]
                )
                both.append(dx.reshape(8, 1, 8, LANES))
            parts.append(jnp.concatenate(both, axis=1).reshape(128, LANES))
        rows = jnp.concatenate(parts, axis=0)
        for h, buf in enumerate(bufs):
            buf[pl.ds(pj, 256, stride=2), :] = rows[:, 128 * h : 128 * h + 128]
    for h, buf in enumerate(bufs):
        out_ref[:, :, :, 128 * h : 128 * h + 128] = buf[...].astype(BF).reshape(2, 16, 16, 128)


def norm_backward(planes, own, got, gain, bias, stat):
    vec = pl.BlockSpec((1, LANES), lambda c: (0, c))
    block = pl.BlockSpec((4, 128, LANES), lambda c: (0, 0, c))
    return call(
        norm_back_body,
        (arr((2, 16, 16, CIN), BF),),
        (planes, own, got, gain.reshape(1, CIN), bias.reshape(1, CIN), stat),
        flops=COST_BACK,
        scratch=(pltpu.VMEM((512, 128), F32),) * (LANES // 128),
        grid=(CIN // LANES,),
        specs=[block, block, block, vec, vec, pl.BlockSpec((2, 8, LANES), lambda c: (0, 0, c))],
        out_specs=(pl.BlockSpec((2, 16, 16, LANES), lambda c: (0, 0, 0, c)),),
    )[0]


def shifted(cot, si, sj):
    row = lax.broadcasted_iota(jnp.int32, cot.shape, 0)
    value = cot
    if sj:
        value = jnp.where(row % 8 == 7, 0.0, pltpu.roll(value, cot.shape[0] - 1, 0))
    if si:
        value = jnp.where((row // 8) % 8 == 7, 0.0, pltpu.roll(value, cot.shape[0] - 8, 0))
    return value


def delayed(acc, si, sj):
    row = lax.broadcasted_iota(jnp.int32, acc.shape, 0)
    value = acc
    if sj:
        value = jnp.where(row % 8 == 0, 0.0, pltpu.roll(value, 1, 0))
    if si:
        value = jnp.where((row // 8) % 8 == 0, 0.0, pltpu.roll(value, 8, 0))
    return value


def cot_rows(own_ref, got_ref):
    return jnp.concatenate([own_ref[...], got_ref[...]], axis=0).astype(F32)


def last_tap(z):
    return -(-(z + 1) * 2304 // CIN) - 1


def wgrad_body(act_own, act_got, cot_own, cot_got, *refs):
    outs = refs[:4]
    whole, tail, turned, sem = refs[4:8]
    x, _, _, core = position()
    cot = cot_rows(cot_own, cot_got)
    moved = {(si, sj): shifted(cot, si, sj).astype(BF) for si in range(2) for sj in range(2)}
    copies = []

    def send(src, dst):
        copies.append(pltpu.make_async_copy(src, dst, sem.at[len(copies)]))
        copies[-1].start()

    bias = jnp.sum(cot, axis=0, keepdims=True)
    high = bias.astype(BF).astype(F32)
    row = lax.broadcasted_iota(jnp.int32, (CHUNK, HALF), 0)
    tail[...] = jnp.zeros_like(tail)
    tail[0, 0] = jnp.where(row == 0, high, jnp.where(row == 1, bias - high, 0.0)).astype(BF)
    for d in range(4):
        send(tail, outs[d].at[pl.ds(16, 1)])
    ready = set()
    for t, (ky, kx) in enumerate(TAPS):
        (pi, si), (pj, sj) = source(ky), source(kx)
        p = 2 * pi + pj
        if p not in ready:
            turned[p, :, :128] = act_own[p].T
            turned[p, :, 128:] = act_got[p].T
            ready.add(p)
        grad = jnp.dot(turned[p], moved[si, sj], preferred_element_type=F32).astype(BF)
        for q in range(16):
            n = t * 64 + 4 * q
            r, k = n // PER_CHIP, n % PER_CHIP
            whole[r, k : k + 4] = grad[64 * q : 64 * q + 64].reshape(4, CHUNK, HALF)
        for z in range(4):
            if last_tap(z) != t:
                continue
            for d in range(4):
                there = turn(x, d, core)
                send(
                    whole.at[pl.ds(4 * z, 4), pl.ds(QUARTER * there, QUARTER)],
                    outs[d].at[pl.ds(4 * z, 4)],
                )
    for copy in copies:
        copy.wait()


def wgrad(act_own, act_got, cot_own, cot_got):
    vm = pl.BlockSpec(memory_space=pltpu.VMEM)
    hbm = pl.BlockSpec(memory_space=pl.ANY)
    return call(
        wgrad_body,
        (arr((17, QUARTER, CHUNK, HALF), BF),) * 4,
        (act_own, act_got, cot_own, cot_got),
        flops=COST_WGRAD,
        scratch=(
            pltpu.VMEM((16, PER_CHIP, CHUNK, HALF), BF),
            pltpu.VMEM((1, QUARTER, CHUNK, HALF), BF),
            pltpu.VMEM((4, CIN, 256), BF),
            pltpu.SemaphoreType.DMA((20,)),
        ),
        specs=[vm] * 4,
        out_specs=(hbm,) * 4,
        vmem=24,
    )


def conv_body(*refs):
    parts = refs[:4]
    act_own, act_got, cot_own, cot_got, cbias = refs[4:9]
    out_own, out_other, dact_own, dact_other = refs[9:13]
    whole, sem = refs[13], refs[14]
    _, y, _, core = position()
    copies = [
        [
            pltpu.make_async_copy(
                parts[d].at[z],
                whole.at[z, turn(y, d, core)],
                sem.at[4 * z + d],
            )
            for d in range(4)
        ]
        for z in range(4)
    ]
    for group in copies:
        for copy in group:
            copy.start()
    cot = cot_rows(cot_own, cot_got)
    moved = {(si, sj): shifted(cot, si, sj).astype(BF) for si in range(2) for sj in range(2)}

    def tap(t):
        rows = []
        for q in range(16):
            n = t * 64 + 4 * q
            r, k = n // PER_CHIP, n % PER_CHIP
            rows.append(whole[r // 4, r % 4, k : k + 4].reshape(64, HALF))
        return jnp.concatenate(rows, axis=0)

    total = jnp.broadcast_to(cbias[...], (256, HALF))
    here = 0
    for t, (ky, kx) in enumerate(TAPS):
        while here < 4 and here * 2304 < (t + 1) * CIN:
            for copy in copies[here]:
                copy.wait()
            here += 1
        (pi, si), (pj, sj) = source(ky), source(kx)
        act = jnp.concatenate([act_own[2 * pi + pj], act_got[2 * pi + pj]], axis=0)
        term = jnp.dot(act, tap(t), preferred_element_type=F32)
        total = total + delayed(term, si, sj)
    result = total.astype(BF)
    out_own[...] = result[:128]
    out_other[...] = result[128:]
    for pi in range(2):
        for pj in range(2):
            acc = None
            for t, (ky, kx) in enumerate(TAPS):
                (a, si), (b, sj) = source(ky), source(kx)
                if (a, b) != (pi, pj):
                    continue
                term = lax.dot_general(
                    moved[si, sj], tap(t), (((1,), (1,)), ((), ())), preferred_element_type=F32
                )
                acc = term if acc is None else acc + term
            dact_own[2 * pi + pj] = acc[:128]
            dact_other[2 * pi + pj] = acc[128:].astype(BF)


def conv(parts, act_own, act_got, cot_own, cot_got, cbias):
    vm = pl.BlockSpec(memory_space=pltpu.VMEM)
    hbm = pl.BlockSpec(memory_space=pl.ANY)
    out = arr((128, HALF), BF)
    return call(
        conv_body,
        (out, out, arr((4, 128, CIN), F32), arr((4, 128, CIN), BF)),
        (*parts, act_own, act_got, cot_own, cot_got, cbias),
        flops=COST_CONV,
        scratch=(
            pltpu.VMEM((4, 4, PER_CHIP, CHUNK, HALF), BF),
            pltpu.SemaphoreType.DMA((16,)),
        ),
        specs=[hbm] * 4 + [vm] * 5,
        out_specs=(vm,) * 4,
        vmem=32,
    )


def block_body(rows, theirs, out):
    core = position()[3]
    own = jnp.where(core == 0, rows[:, :, :HALF], rows[:, :, HALF:])
    out[pl.ds(18 * core, 18)] = own
    out[pl.ds(18 * (1 - core), 18)] = theirs[...]


def spread_z_body(a0, a1, a2, a3, _, out):
    _, _, z, core = position()
    for d, ref in enumerate((a0, a1, a2, a3)):
        out[turn(z, d, core)] = ref[...]


def gather_kernel(kernel, core, grads):
    vm = pl.BlockSpec(memory_space=pltpu.VMEM)
    anywhere = pl.BlockSpec(memory_space=pl.ANY)
    rows = kernel.reshape(18, CHUNK, COUT)
    theirs = fetch(jnp.where(core == 0, rows[:, :, HALF:], rows[:, :, :HALF]), swap=1)
    block = call(
        block_body,
        (arr((PER_CHIP, CHUNK, HALF), BF),),
        (rows, theirs),
    )[0]
    got = [block] + [fetch(block, dz=2 * d) for d in range(1, 4)]
    level = call(
        spread_z_body,
        (arr((4, PER_CHIP, CHUNK, HALF), BF),),
        (*got, grads),
        specs=[vm] * 4 + [anywhere],
    )[0]
    parts = [level]
    for _ in range(3):
        parts.append(fetch(parts[-1], dy=1))
    return parts


def four(refs, index):
    v = [ref[index].astype(F32) for ref in refs]
    return (v[0] + v[2]) + (v[1] + v[3])


def bias_four(refs, index):
    v = [ref[index].astype(F32) for ref in refs]
    v = [w[0:1] + w[1:2] for w in v]
    return (v[0] + v[2]) + (v[1] + v[3])


def bias_chunk(total):
    high = total.astype(BF).astype(F32)
    row = lax.broadcasted_iota(jnp.int32, (CHUNK, HALF), 0)
    return jnp.where(row == 0, high, jnp.where(row == 1, total - high, 0.0)).astype(BF)


def sum_x_body(*refs):
    ins, outs = refs[:4], refs[4:]
    _, y, _, core = position()
    bias = bias_chunk(bias_four(ins, (16, 0)))
    for d in range(4):
        there = turn(y, d, core)
        for z in range(4):
            outs[d][QUARTER * z : QUARTER * z + QUARTER] = four(ins, 4 * z + there).astype(BF)
        outs[d][4 * QUARTER] = bias


def sum_y_body(*refs):
    ins, outs = refs[:4], refs[4:]
    _, _, z, core = position()
    bias = bias_chunk(bias_four(ins, 4 * QUARTER))
    for d in range(4):
        there = turn(z, d, core)
        outs[d][:QUARTER] = four(ins, pl.ds(QUARTER * there, QUARTER)).astype(BF)
        outs[d][QUARTER] = bias


def sum_z_body(*refs):
    ins, out = refs[:4], refs[4]
    out[:QUARTER] = four(ins, pl.ds(0, QUARTER))
    row = lax.broadcasted_iota(jnp.int32, (CHUNK, HALF), 0)
    out[QUARTER] = jnp.where(row == 0, bias_four(ins, QUARTER), 0.0)


def place_body(f0, f1, f2, f3, mine, theirs, whole):
    x, _, _, core = position()
    for d, ref in enumerate((f0, f1, f2, f3)):
        whole[pl.ds(QUARTER * turn(x, d, core), QUARTER)] = ref[:QUARTER]
    mine[:18] = whole[pl.ds(18 * core, 18)]
    theirs[:18] = whole[pl.ds(18 * (1 - core), 18)]
    mine[18] = f0[QUARTER]
    theirs[18] = f0[QUARTER]


def reduce_gradient(got, core):
    send = call(
        sum_x_body,
        (arr((4 * QUARTER + 1, CHUNK, HALF), BF),) * 4,
        got,
        flops=COST_SUM,
        vmem=16,
    )
    got = [send[0]] + [fetch(send[4 - d], dy=d) for d in range(1, 4)]
    send = call(sum_y_body, (arr((QUARTER + 1, CHUNK, HALF), BF),) * 4, got, flops=COST_SUM)
    got = [send[0]] + [fetch(send[4 - d], dz=2 * d) for d in range(1, 4)]
    part = call(sum_z_body, (arr((QUARTER + 1, CHUNK, HALF), F32),), got, flops=COST_SUM)[0]
    full = (part + pair_low(part)) * (1.0 / IMAGES)
    rows = full[:QUARTER]
    every = [full] + [fetch(rows, dx=d) for d in range(1, 4)]
    mine, theirs = call(
        place_body,
        (arr((19, CHUNK, HALF), F32),) * 2,
        every,
        scratch=(pltpu.VMEM((PER_CHIP, CHUNK, HALF), F32),),
    )
    got = fetch(theirs, swap=1)
    both = jnp.where(
        core == 0, jnp.concatenate([mine, got], axis=-1), jnp.concatenate([got, mine], axis=-1)
    )
    return both[:18].reshape(288, COUT), both[18, 0]


def local(images, kernel, gn_gain, gn_bias, conv_bias, cotangent):
    core = position()[3]
    cot = cotangent.reshape(128, COUT)
    left, right = cot[:, :HALF], cot[:, HALF:]
    cot_own = jnp.where(core == 0, left, right)
    cot_got = fetch(jnp.where(core == 0, right, left), swap=1)
    act, planes, stat = norm_forward(images, gn_gain, gn_bias)
    act_got = fetch(act, swap=1)
    send = wgrad(act, act_got, cot_own, cot_got)
    got = [send[0]] + [fetch(send[4 - d], dx=d) for d in range(1, 4)]
    parts = gather_kernel(kernel, core, send[0])
    kernel_grad, bias_grad = reduce_gradient(got, core)
    cbias = jnp.where(core == 0, conv_bias[:HALF], conv_bias[HALF:]).reshape(1, HALF)
    out_own, out_other, dact_own, dact_other = conv(
        parts, act, act_got, cot_own, cot_got, cbias
    )
    dact_got = fetch(dact_other, swap=1)
    out_got = fetch(out_other, swap=1)
    outputs = jnp.where(
        core == 0,
        jnp.concatenate([out_own, out_got], axis=-1),
        jnp.concatenate([out_got, out_own], axis=-1),
    ).reshape(cotangent.shape)
    input_grad = norm_backward(planes, dact_own, dact_got, gn_gain, gn_bias, stat)
    return outputs, input_grad, kernel_grad, bias_grad


def solution(mesh):
    return jax.shard_map(
        local,
        mesh=mesh,
        in_specs=(
            P(AXES, None, None, None),
            P("shard", None),
            P(),
            P(),
            P(),
            P(AXES, None, None, None),
        ),
        out_specs=(
            P(AXES, None, None, None),
            P(AXES, None, None, None),
            P("shard", None),
            P(),
        ),
        check_vma=False,
    )
```

```python
import functools

import jax
import jax.numpy as jnp
from jax import lax
from jax.experimental import pallas as pl
from jax.experimental.pallas import tpu as pltpu
from jax.sharding import PartitionSpec as P

BF = jnp.bfloat16
F32 = jnp.float32
AXES = ("rep", "shard")
CIN, COUT, HALF = 1024, 512, 256
GSIZE = 32
LANES = 256
IMAGES = 512
EPS = 1e-05
MIB = 1024 * 1024
CHUNK, PER_CHIP, QUARTER = 16, 36, 9
COST_NORM, COST_WGRAD, COST_CONV, COST_BACK, COST_SUM, COST_SPREAD, COST_MARK = 10**10, 2 * 10**10, 10**10, 10**9, 10**10, 10**10, 3 * 10**10
MOVED_CONV, MOVED_BACK, COST_PLACE = 0, 0, 2 * 10**10
TAPS = [(ky, kx) for ky in range(3) for kx in range(3)]


def source(k):
    return (0, 0) if k == 1 else (1, 1 if k == 0 else 0)


def position():
    rep, shard = lax.axis_index("rep"), lax.axis_index("shard")
    return lax.rem(rep, 4), lax.rem(shard // 2, 4), shard // 8, lax.rem(shard, 2)


def number(x, y, z, core):
    return ((z % 2) * 4 + x) * 32 + ((z // 2) * 4 + y) * 2 + core


@functools.lru_cache(maxsize=None)
def pairs(dx, dy, dz, swap):
    out = []
    for x in range(4):
        for y in range(4):
            for z in range(8):
                for core in range(2):
                    sign = 1 - 2 * core
                    src = number(
                        (x + sign * dx) % 4, (y + sign * dy) % 4, (z + sign * dz) % 8, core ^ swap
                    )
                    out.append((src, number(x, y, z, core)))
    return sorted(out)


def fetch(value, dx=0, dy=0, dz=0, swap=0):
    with jax.named_scope(f"from_x{dx}_y{dy}_z{dz}_core{swap}"):
        return lax.ppermute(value, AXES, pairs(dx, dy, dz, swap))


def pair_low(value):
    out = []
    for x in range(4):
        for y in range(4):
            for z in range(8):
                for core in range(2):
                    out.append((number(x, y, z ^ 1, core), number(x, y, z, core)))
    with jax.named_scope("from_z_low"):
        return lax.ppermute(value, AXES, sorted(out))


def turn(index, step, core):
    return lax.rem(index + jnp.where(core == 0, step, 4 - step), 4)


def call(body, outs, args, flops=0, moved=None, scratch=(), specs=None, out_specs=None, grid=None, vmem=8, after=(), **kw):
    if after:
        inner, count = body, len(args)
        body = lambda *refs: inner(*refs[:count], *refs[count + len(after) :])
        if specs is None:
            specs = [pl.BlockSpec(memory_space=pltpu.VMEM)] * count
        specs = list(specs) + [pl.BlockSpec(memory_space=pl.ANY)] * len(after)
        args = (*args, *after)
    if moved is None:
        moved = sum(a.size * a.dtype.itemsize for a in (*args[: len(args) - len(after)], *outs))
    params = dict(kw)
    if grid is not None:
        params["grid"] = grid
    if specs is not None:
        params["in_specs"] = specs
    if out_specs is not None:
        params["out_specs"] = out_specs
    return pl.pallas_call(
        body,
        out_shape=outs,
        scratch_shapes=list(scratch),
        compiler_params=pltpu.CompilerParams(vmem_limit_bytes=vmem * MIB),
        cost_estimate=pl.CostEstimate(flops=flops, bytes_accessed=moved, transcendentals=0),
        **params,
    )(*args)


def arr(shape, dtype):
    return jax.ShapeDtypeStruct(shape, dtype)


def group_mean(rows):
    a = lax.broadcasted_iota(jnp.int32, (LANES, LANES), 0) // GSIZE
    b = lax.broadcasted_iota(jnp.int32, (LANES, LANES), 1) // GSIZE
    ones = jnp.where(a == b, 1.0, 0.0).astype(F32)
    total = lax.dot_general(
        rows,
        ones,
        (((1,), (0,)), ((), ())),
        precision=lax.Precision.HIGHEST,
        preferred_element_type=F32,
    )
    return total * (1.0 / (256 * GSIZE))


def stack_rows(a, b):
    row = lax.broadcasted_iota(jnp.int32, (8, LANES), 0)
    return jnp.where(row == 0, a, jnp.where(row == 1, b, 0.0))


def norm_body(x_ref, gain_ref, bias_ref, act_ref, plane_ref, stat_ref, *bufs):
    x = x_ref[...].astype(F32).reshape(2, 256, LANES)
    sums = [jnp.sum(x[i], axis=0, keepdims=True) for i in range(2)]
    mean = group_mean(stack_rows(*sums))
    sq = [jnp.sum(jnp.square(x[i] - mean[i : i + 1]), axis=0, keepdims=True) for i in range(2)]
    rstd = lax.rsqrt(group_mean(stack_rows(*sq)) + EPS)
    stat_ref[0] = mean
    stat_ref[1] = rstd
    for h, buf in enumerate(bufs):
        buf[...] = x[:, :, 128 * h : 128 * h + 128].reshape(512, 128)
    gain, bias = gain_ref[...], bias_ref[...]
    for pj in range(2):
        part = jnp.concatenate([buf[pl.ds(pj, 256, stride=2), :] for buf in bufs], axis=-1)
        part = part.reshape(2, 8, 2, 8, LANES)
        for pi in range(2):
            for i in range(2):
                xp = part[i, :, pi].reshape(64, LANES)
                y = (xp - mean[i : i + 1]) * rstd[i : i + 1] * gain + bias
                rows = slice(64 * i, 64 * i + 64)
                act_ref[2 * pi + pj, rows, :] = (y * jax.nn.sigmoid(y)).astype(BF)
                plane_ref[2 * pi + pj, rows, :] = xp.astype(BF)


def norm_forward(images, gain, bias, after):
    plane = arr((4, 128, CIN), BF)
    vec = pl.BlockSpec((1, LANES), lambda c: (0, c))
    block = pl.BlockSpec((4, 128, LANES), lambda c: (0, 0, c))
    return call(
        norm_body,
        (plane, plane, arr((2, 8, CIN), F32)),
        (images, gain.reshape(1, CIN), bias.reshape(1, CIN)),
        flops=COST_NORM,
        scratch=(pltpu.VMEM((512, 128), F32),) * (LANES // 128),
        grid=(CIN // LANES,),
        specs=[pl.BlockSpec((2, 16, 16, LANES), lambda c: (0, 0, 0, c)), vec, vec],
        out_specs=(block, block, pl.BlockSpec((2, 8, LANES), lambda c: (0, 0, c))),
        after=after,
    )


def norm_back_body(
    xp_ref, own_ref, got_ref, gain_ref, bias_ref, stat_ref, res_own, res_got, out_ref, res_ref, mark, *bufs
):
    core = position()[3]
    for c in range(2):
        res_ref[:, HALF * c : HALF * c + HALF] = jnp.where(core == c, res_own[...], res_got[...])
    mark[...] = jnp.zeros_like(mark)
    gain, bias = gain_ref[...], bias_ref[...]
    mean, rstd = stat_ref[0], stat_ref[1]
    hats, grads, one, two = [], [], [], []
    for i in range(2):
        rows = slice(64 * i, 64 * i + 64)
        m, r = mean[i : i + 1], rstd[i : i + 1]
        h_list, g_list, s1, s2 = [], [], 0.0, 0.0
        for p in range(4):
            hat = (xp_ref[p, rows, :].astype(F32) - m) * r
            y = hat * gain + bias
            s = jax.nn.sigmoid(y)
            d = own_ref[p, rows, :] + got_ref[p, rows, :].astype(F32)
            g = d * (s * (1.0 + y * (1.0 - s))) * gain
            s1 = s1 + jnp.sum(g, axis=0, keepdims=True)
            s2 = s2 + jnp.sum(g * hat, axis=0, keepdims=True)
            h_list.append(hat)
            g_list.append(g)
        hats.append(h_list)
        grads.append(g_list)
        one.append(s1)
        two.append(s2)
    mean1 = group_mean(stack_rows(*one))
    mean2 = group_mean(stack_rows(*two))
    for pj in range(2):
        parts = []
        for i in range(2):
            both = []
            for pi in range(2):
                p = 2 * pi + pj
                dx = rstd[i : i + 1] * (
                    grads[i][p] - mean1[i : i + 1] - hats[i][p] * mean2[i : i + 1]
                )
                both.append(dx.reshape(8, 1, 8, LANES))
            parts.append(jnp.concatenate(both, axis=1).reshape(128, LANES))
        rows = jnp.concatenate(parts, axis=0)
        for h, buf in enumerate(bufs):
            buf[pl.ds(pj, 256, stride=2), :] = rows[:, 128 * h : 128 * h + 128]
    for h, buf in enumerate(bufs):
        out_ref[:, :, :, 128 * h : 128 * h + 128] = buf[...].astype(BF).reshape(2, 16, 16, 128)


def norm_backward(planes, own, got, gain, bias, stat, res_own, res_got):
    vec = pl.BlockSpec((1, LANES), lambda c: (0, c))
    block = pl.BlockSpec((4, 128, LANES), lambda c: (0, 0, c))
    return call(
        norm_back_body,
        (arr((2, 16, 16, CIN), BF), arr((128, COUT), BF), arr((8, 128), F32)),
        (planes, own, got, gain.reshape(1, CIN), bias.reshape(1, CIN), stat, res_own, res_got),
        flops=COST_BACK,
        moved=MOVED_BACK,
        scratch=(pltpu.VMEM((512, 128), F32),) * (LANES // 128),
        grid=(CIN // LANES,),
        specs=[block, block, block, vec, vec, pl.BlockSpec((2, 8, LANES), lambda c: (0, 0, c))]
        + [pl.BlockSpec((128, HALF), lambda c: (0, 0))] * 2,
        out_specs=(
            pl.BlockSpec((2, 16, 16, LANES), lambda c: (0, 0, 0, c)),
            pl.BlockSpec((128, COUT), lambda c: (0, 0)),
            pl.BlockSpec((8, 128), lambda c: (0, 0)),
        ),
    )


def shifted(cot, si, sj):
    row = lax.broadcasted_iota(jnp.int32, cot.shape, 0)
    value = cot
    if sj:
        value = jnp.where(row % 8 == 7, 0.0, pltpu.roll(value, cot.shape[0] - 1, 0))
    if si:
        value = jnp.where((row // 8) % 8 == 7, 0.0, pltpu.roll(value, cot.shape[0] - 8, 0))
    return value


def delayed(acc, si, sj):
    row = lax.broadcasted_iota(jnp.int32, acc.shape, 0)
    value = acc
    if sj:
        value = jnp.where(row % 8 == 0, 0.0, pltpu.roll(value, 1, 0))
    if si:
        value = jnp.where((row // 8) % 8 == 0, 0.0, pltpu.roll(value, 8, 0))
    return value


def cot_rows(own_ref, got_ref):
    return jnp.concatenate([own_ref[...], got_ref[...]], axis=0).astype(F32)


def last_tap(z):
    return -(-(z + 1) * 2304 // CIN) - 1


def wgrad_body(act_own, act_got, cot_own, cot_got, *refs):
    ahead, here, behind, far_low, far_high, bias = refs[:6]
    whole, turned, sem = refs[6:9]
    x, _, _, core = position()
    cot = cot_rows(cot_own, cot_got)
    moved = {(si, sj): shifted(cot, si, sj).astype(BF) for si in range(2) for sj in range(2)}
    bias[...] = jnp.broadcast_to(jnp.sum(cot, axis=0, keepdims=True), bias.shape)
    copies = []
    ready = set()
    for t, (ky, kx) in enumerate(TAPS):
        (pi, si), (pj, sj) = source(ky), source(kx)
        p = 2 * pi + pj
        if p not in ready:
            turned[p, :, :128] = act_own[p].T
            turned[p, :, 128:] = act_got[p].T
            ready.add(p)
        grad = jnp.dot(turned[p], moved[si, sj], preferred_element_type=F32).astype(BF)
        for q in range(16):
            n = t * 64 + 4 * q
            r, k = n // PER_CHIP, n % PER_CHIP
            whole[r, k : k + 4] = grad[64 * q : 64 * q + 64].reshape(4, CHUNK, HALF)
        for z in range(4):
            if last_tap(z) != t:
                continue
            far = far_low if z < 2 else far_high
            for d, (out, at) in enumerate(((here, z), (ahead, z), (far, z % 2), (behind, z))):
                copies.append(
                    pltpu.make_async_copy(
                        whole.at[pl.ds(4 * z, 4), pl.ds(QUARTER * turn(x, d, core), QUARTER)],
                        out.at[pl.ds(4 * at, 4)],
                        sem.at[len(copies)],
                    )
                )
                copies[-1].start()
    for copy in copies:
        copy.wait()


def wgrad(act_own, act_got, cot_own, cot_got):
    vm = pl.BlockSpec(memory_space=pltpu.VMEM)
    hbm = pl.BlockSpec(memory_space=pl.ANY)
    full = arr((16, QUARTER, CHUNK, HALF), BF)
    half = arr((8, QUARTER, CHUNK, HALF), BF)
    return call(
        wgrad_body,
        (full, full, full, half, half, arr((8, HALF), F32)),
        (act_own, act_got, cot_own, cot_got),
        flops=COST_WGRAD,
        scratch=(
            pltpu.VMEM((16, PER_CHIP, CHUNK, HALF), BF),
            pltpu.VMEM((4, CIN, 256), BF),
            pltpu.SemaphoreType.DMA((16,)),
        ),
        specs=[vm] * 4,
        out_specs=(hbm,) * 5 + (vm,),
        vmem=24,
    )


def conv_body(*refs):
    here, ahead, behind, far_low, far_high = refs[:5]
    act_own, act_got, cot_own, cot_got, cbias = refs[5:10]
    out_own, out_other, dact_own, dact_other = refs[10:14]
    whole, sem = refs[14], refs[15]
    _, y, _, core = position()
    copies = []
    for z in range(4):
        far = far_low if z < 2 else far_high
        copies.append([])
        for d, part in enumerate((here.at[z], ahead.at[z], far.at[z % 2], behind.at[z])):
            copies[z].append(
                pltpu.make_async_copy(part, whole.at[z, turn(y, d, core)], sem.at[4 * z + d])
            )
    for group in copies:
        for copy in group:
            copy.start()
    cot = cot_rows(cot_own, cot_got)
    moved = {(si, sj): shifted(cot, si, sj).astype(BF) for si in range(2) for sj in range(2)}

    def tap(t):
        rows = []
        for q in range(16):
            n = t * 64 + 4 * q
            r, k = n // PER_CHIP, n % PER_CHIP
            rows.append(whole[r // 4, r % 4, k : k + 4].reshape(64, HALF))
        return jnp.concatenate(rows, axis=0)

    total = jnp.broadcast_to(cbias[...], (256, HALF))
    row = 0
    for t, (ky, kx) in enumerate(TAPS):
        while row < 4 and row * 2304 < (t + 1) * CIN:
            for copy in copies[row]:
                copy.wait()
            row += 1
        (pi, si), (pj, sj) = source(ky), source(kx)
        act = jnp.concatenate([act_own[2 * pi + pj], act_got[2 * pi + pj]], axis=0)
        term = jnp.dot(act, tap(t), preferred_element_type=F32)
        total = total + delayed(term, si, sj)
    result = total.astype(BF)
    out_own[...] = result[:128]
    out_other[...] = result[128:]
    for pi in range(2):
        for pj in range(2):
            acc = None
            for t, (ky, kx) in enumerate(TAPS):
                (a, si), (b, sj) = source(ky), source(kx)
                if (a, b) != (pi, pj):
                    continue
                term = lax.dot_general(
                    moved[si, sj], tap(t), (((1,), (1,)), ((), ())), preferred_element_type=F32
                )
                acc = term if acc is None else acc + term
            dact_own[2 * pi + pj] = acc[:128]
            dact_other[2 * pi + pj] = acc[128:].astype(BF)


def conv(parts, act_own, act_got, cot_own, cot_got, cbias, after):
    vm = pl.BlockSpec(memory_space=pltpu.VMEM)
    hbm = pl.BlockSpec(memory_space=pl.ANY)
    out = arr((128, HALF), BF)
    return call(
        conv_body,
        (out, out, arr((4, 128, CIN), F32), arr((4, 128, CIN), BF)),
        (*parts, act_own, act_got, cot_own, cot_got, cbias),
        flops=COST_CONV,
        moved=MOVED_CONV,
        scratch=(
            pltpu.VMEM((4, 4, PER_CHIP, CHUNK, HALF), BF),
            pltpu.SemaphoreType.DMA((16,)),
        ),
        specs=[hbm] * 5 + [vm] * 5,
        out_specs=(vm,) * 4,
        vmem=32,
        after=after,
    )


def block_body(rows, theirs, out):
    core = position()[3]
    own = jnp.where(core == 0, rows[:, :, :HALF], rows[:, :, HALF:])
    out[pl.ds(18 * core, 18)] = own
    out[pl.ds(18 * (1 - core), 18)] = theirs[...]


def spread_z_body(a0, a2, a1, a3, out):
    _, _, z, core = position()
    for d, ref in enumerate((a0, a1, a2, a3)):
        out[turn(z, d, core)] = ref[...]


def chip_block(kernel, core):
    rows = kernel.reshape(18, CHUNK, COUT)
    theirs = fetch(jnp.where(core == 0, rows[:, :, HALF:], rows[:, :, :HALF]), swap=1)
    return call(block_body, (arr((PER_CHIP, CHUNK, HALF), BF),), (rows, theirs))[0]


def mark_body(out):
    out[...] = jnp.zeros_like(out)


def gather_z(block):
    got = [block] + [fetch(block, dz=2 * d) for d in (2, 1, 3)]
    mark = call(mark_body, (arr((8, 128), F32),), (), flops=COST_MARK, after=(got[2],))[0]
    return mark, call(spread_z_body, (arr((4, PER_CHIP, CHUNK, HALF), BF),), got, flops=COST_SPREAD)[0]


def across_body(ahead, behind, low, high):
    low[...] = ahead[:2]
    high[...] = behind[2:]


def gather_y(level, ahead, behind, after):
    low, high = call(
        across_body,
        (arr((2, PER_CHIP, CHUNK, HALF), BF),) * 2,
        (ahead, behind),
        vmem=12,
        after=after,
    )
    return level, ahead, behind, fetch(low, dy=1), fetch(high, dy=3)


def four(refs, index):
    v = [ref[index].astype(F32) for ref in refs]
    return (v[0] + v[2]) + (v[1] + v[3])


def bias_four(refs, index):
    v = [ref[index].astype(F32) for ref in refs]
    v = [w[0:1] + w[1:2] for w in v]
    return (v[0] + v[2]) + (v[1] + v[3])


def bias_chunk(total):
    high = total.astype(BF).astype(F32)
    row = lax.broadcasted_iota(jnp.int32, (CHUNK, HALF), 0)
    return jnp.where(row == 0, high, jnp.where(row == 1, total - high, 0.0)).astype(BF)


def pass_on_body(ahead, behind, low, high, ahead_out, behind_out):
    ahead_out[:8] = (ahead[:8].astype(F32) + low[...].astype(F32)).astype(BF)
    ahead_out[8:] = ahead[8:]
    behind_out[:8] = behind[:8]
    behind_out[8:] = (behind[8:].astype(F32) + high[...].astype(F32)).astype(BF)


def sum_x_body(own, left, right, bias_ref, *outs):
    _, y, _, core = position()
    bias = bias_chunk(bias_ref[0:1])
    for d in range(4):
        there = turn(y, d, core)
        for z in range(4):
            r = 4 * z + there
            total = own[r].astype(F32) + (left[r].astype(F32) + right[r].astype(F32))
            outs[d][QUARTER * z : QUARTER * z + QUARTER] = total.astype(BF)
        outs[d][4 * QUARTER] = bias


def sum_y_body(*refs):
    ins, outs = refs[:4], refs[4:]
    _, _, z, core = position()
    bias = bias_chunk(bias_four(ins, 4 * QUARTER))
    for d in range(4):
        there = turn(z, d, core)
        outs[d][:QUARTER] = four(ins, pl.ds(QUARTER * there, QUARTER)).astype(BF)
        outs[d][QUARTER] = bias


def sum_z_body(*refs):
    ins, out = refs[:4], refs[4]
    out[:QUARTER] = four(ins, pl.ds(0, QUARTER))
    row = lax.broadcasted_iota(jnp.int32, (CHUNK, HALF), 0)
    out[QUARTER] = jnp.where(row == 0, bias_four(ins, QUARTER), 0.0)


def place_body(*refs):
    ins, (mine, theirs, whole) = refs[:4], refs[4:]
    x, _, _, core = position()
    for d, ref in enumerate(ins):
        whole[pl.ds(QUARTER * turn(x, d, core), QUARTER)] = ref[:QUARTER]
    mine[:18] = whole[pl.ds(18 * core, 18)]
    theirs[:18] = whole[pl.ds(18 * (1 - core), 18)]
    bias = four(ins, QUARTER)
    mine[18] = bias
    theirs[18] = bias


def finish_body(mine, theirs, grad, bias):
    core = position()[3]
    for c in range(2):
        part = jnp.where(core == c, mine[...], theirs[...])
        grad[:, HALF * c : HALF * c + HALF] = part[:18].reshape(288, HALF)
        bias[:, HALF * c : HALF * c + HALF] = part[18, 0:1]


def reduce_xy(parts, mark, around):
    ahead, here, behind, far_low, far_high, bias = parts
    low, high = fetch(far_low, dx=3), fetch(far_high, dx=1)
    ahead, behind = call(
        pass_on_body,
        (arr((16, QUARTER, CHUNK, HALF), BF),) * 2,
        (ahead, behind, low, high),
        flops=COST_SUM,
        vmem=16,
        after=(mark,),
    )
    send = call(
        sum_x_body,
        (arr((4 * QUARTER + 1, CHUNK, HALF), BF),) * 4,
        (here, fetch(ahead, dx=3), fetch(behind, dx=1), bias),
        flops=COST_SUM,
        vmem=16,
    )
    got = [send[0]] + [fetch(send[4 - d], dy=d) for d in range(1, 4)]
    return call(
        sum_y_body,
        (arr((QUARTER + 1, CHUNK, HALF), BF),) * 4,
        got,
        flops=COST_SUM,
        after=around,
    )


def reduce_z(send):
    got = [send[0]] + [fetch(send[4 - d], dz=2 * d) for d in range(1, 4)]
    part = call(sum_z_body, (arr((QUARTER + 1, CHUNK, HALF), F32),), got, flops=COST_SUM)[0]
    return (part + pair_low(part)) * (1.0 / IMAGES)


def spread_x(full, last):
    every = [full] + [fetch(full, dx=d) for d in range(1, 4)]
    mine, theirs = call(
        place_body,
        (arr((19, CHUNK, HALF), F32),) * 2,
        every,
        flops=COST_PLACE,
        scratch=(pltpu.VMEM((PER_CHIP, CHUNK, HALF), F32),),
    )
    grad, bias = call(
        finish_body,
        (arr((288, COUT), F32), arr((1, COUT), F32)),
        (mine, fetch(theirs, swap=1)),
        after=(last,),
    )
    return grad, bias.reshape(COUT)


def local(images, kernel, gn_gain, gn_bias, conv_bias, cotangent):
    core = position()[3]
    cot = cotangent.reshape(128, COUT)
    left, right = cot[:, :HALF], cot[:, HALF:]
    cot_own = jnp.where(core == 0, left, right)
    cot_got = fetch(jnp.where(core == 0, right, left), swap=1)
    block = chip_block(kernel, core)
    act, planes, stat = norm_forward(images, gn_gain, gn_bias, (block,))
    act_got = fetch(act, swap=1)
    grads = wgrad(act, act_got, cot_own, cot_got)
    mark, level = gather_z(block)
    around = fetch(level, dy=1), fetch(level, dy=3)
    send = reduce_xy(grads, mark, around)
    parts = gather_y(level, *around, (send[0],))
    cbias = jnp.where(core == 0, conv_bias[:HALF], conv_bias[HALF:]).reshape(1, HALF)
    full = reduce_z(send)
    out_own, out_other, dact_own, dact_other = conv(
        parts, act, act_got, cot_own, cot_got, cbias, (full,)
    )
    dact_got = fetch(dact_other, swap=1)
    out_got = fetch(out_other, swap=1)
    input_grad, outputs, mark = norm_backward(
        planes, dact_own, dact_got, gn_gain, gn_bias, stat, out_own, out_got
    )
    outputs = outputs.reshape(cotangent.shape)
    kernel_grad, bias_grad = spread_x(full, mark)
    return outputs, input_grad, kernel_grad, bias_grad


def solution(mesh):
    return jax.shard_map(
        local,
        mesh=mesh,
        in_specs=(
            P(AXES, None, None, None),
            P("shard", None),
            P(),
            P(),
            P(),
            P(AXES, None, None, None),
        ),
        out_specs=(
            P(AXES, None, None, None),
            P(AXES, None, None, None),
            P("shard", None),
            P(),
        ),
        check_vma=False,
    )
```

```python
import functools

import jax
import jax.numpy as jnp
from jax import lax
from jax.experimental import pallas as pl
from jax.experimental.pallas import tpu as pltpu
from jax.sharding import PartitionSpec as P

BF = jnp.bfloat16
F32 = jnp.float32
AXES = ("rep", "shard")
CIN, COUT, HALF = 1024, 512, 256
GSIZE = 32
LANES = 256
IMAGES = 512
EPS = 1e-05
MIB = 1024 * 1024
CHUNK, PER_CHIP, QUARTER = 16, 36, 9
COST_NORM, COST_WGRAD, COST_CONV, COST_BACK, COST_SUM, COST_SPREAD, COST_MARK = 10**10, 2 * 10**10, 10**10, 10**9, 10**10, 10**10, 3 * 10**10
MOVED_CONV, MOVED_BACK, COST_PLACE = 0, 0, 2 * 10**10
TAPS = [(ky, kx) for ky in range(3) for kx in range(3)]


def source(k):
    return (0, 0) if k == 1 else (1, 1 if k == 0 else 0)


def position():
    rep, shard = lax.axis_index("rep"), lax.axis_index("shard")
    return lax.rem(rep, 4), lax.rem(shard // 2, 4), shard // 8, lax.rem(shard, 2)


def number(x, y, z, core):
    return ((z % 2) * 4 + x) * 32 + ((z // 2) * 4 + y) * 2 + core


@functools.lru_cache(maxsize=None)
def pairs(dx, dy, dz, swap):
    out = []
    for x in range(4):
        for y in range(4):
            for z in range(8):
                for core in range(2):
                    sign = 1 - 2 * core
                    src = number(
                        (x + sign * dx) % 4, (y + sign * dy) % 4, (z + sign * dz) % 8, core ^ swap
                    )
                    out.append((src, number(x, y, z, core)))
    return sorted(out)


def fetch(value, dx=0, dy=0, dz=0, swap=0):
    with jax.named_scope(f"from_x{dx}_y{dy}_z{dz}_core{swap}"):
        return lax.ppermute(value, AXES, pairs(dx, dy, dz, swap))


def pair_low(value):
    out = []
    for x in range(4):
        for y in range(4):
            for z in range(8):
                for core in range(2):
                    out.append((number(x, y, z ^ 1, core), number(x, y, z, core)))
    with jax.named_scope("from_z_low"):
        return lax.ppermute(value, AXES, sorted(out))


def turn(index, step, core):
    return lax.rem(index + jnp.where(core == 0, step, 4 - step), 4)


def call(body, outs, args, flops=0, moved=None, scratch=(), specs=None, out_specs=None, grid=None, vmem=8, after=(), **kw):
    if after:
        inner, count = body, len(args)
        body = lambda *refs: inner(*refs[:count], *refs[count + len(after) :])
        if specs is None:
            specs = [pl.BlockSpec(memory_space=pltpu.VMEM)] * count
        specs = list(specs) + [pl.BlockSpec(memory_space=pl.ANY)] * len(after)
        args = (*args, *after)
    if moved is None:
        moved = sum(a.size * a.dtype.itemsize for a in (*args[: len(args) - len(after)], *outs))
    params = dict(kw)
    if grid is not None:
        params["grid"] = grid
    if specs is not None:
        params["in_specs"] = specs
    if out_specs is not None:
        params["out_specs"] = out_specs
    return pl.pallas_call(
        body,
        out_shape=outs,
        scratch_shapes=list(scratch),
        compiler_params=pltpu.CompilerParams(vmem_limit_bytes=vmem * MIB),
        cost_estimate=pl.CostEstimate(flops=flops, bytes_accessed=moved, transcendentals=0),
        **params,
    )(*args)


def arr(shape, dtype):
    return jax.ShapeDtypeStruct(shape, dtype)


def group_mean(rows):
    a = lax.broadcasted_iota(jnp.int32, (LANES, LANES), 0) // GSIZE
    b = lax.broadcasted_iota(jnp.int32, (LANES, LANES), 1) // GSIZE
    ones = jnp.where(a == b, 1.0, 0.0).astype(F32)
    total = lax.dot_general(
        rows,
        ones,
        (((1,), (0,)), ((), ())),
        precision=lax.Precision.HIGHEST,
        preferred_element_type=F32,
    )
    return total * (1.0 / (256 * GSIZE))


def stack_rows(a, b):
    row = lax.broadcasted_iota(jnp.int32, (8, LANES), 0)
    return jnp.where(row == 0, a, jnp.where(row == 1, b, 0.0))


def norm_body(x_hbm, gain_ref, bias_ref, act_ref, plane_ref, stat_ref, raw, *rest):
    bufs, sem = rest[:2], rest[2]
    count = CIN // LANES
    copies = [
        pltpu.make_async_copy(
            x_hbm.at[:, :, :, pl.ds(LANES * n, LANES)], raw.at[n], sem.at[n]
        )
        for n in range(count)
    ]
    for copy in copies:
        copy.start()
    for n, copy in enumerate(copies):
        lanes = slice(LANES * n, LANES * n + LANES)
        copy.wait()
        x = raw[n].astype(F32).reshape(2, 256, LANES)
        sums = [jnp.sum(x[i], axis=0, keepdims=True) for i in range(2)]
        mean = group_mean(stack_rows(*sums))
        sq = [jnp.sum(jnp.square(x[i] - mean[i : i + 1]), axis=0, keepdims=True) for i in range(2)]
        rstd = lax.rsqrt(group_mean(stack_rows(*sq)) + EPS)
        stat_ref[0, :, lanes] = mean
        stat_ref[1, :, lanes] = rstd
        for h, buf in enumerate(bufs):
            buf[n % 2] = x[:, :, 128 * h : 128 * h + 128].reshape(512, 128)
        gain, bias = gain_ref[:, lanes], bias_ref[:, lanes]
        for pj in range(2):
            part = jnp.concatenate(
                [buf[n % 2, pl.ds(pj, 256, stride=2), :] for buf in bufs], axis=-1
            )
            part = part.reshape(2, 8, 2, 8, LANES)
            for pi in range(2):
                for i in range(2):
                    xp = part[i, :, pi].reshape(64, LANES)
                    y = (xp - mean[i : i + 1]) * rstd[i : i + 1] * gain + bias
                    rows = slice(64 * i, 64 * i + 64)
                    act_ref[2 * pi + pj, rows, lanes] = (y * jax.nn.sigmoid(y)).astype(BF)
                    plane_ref[2 * pi + pj, rows, lanes] = xp.astype(BF)


def norm_forward(images, gain, bias, after):
    vm = pl.BlockSpec(memory_space=pltpu.VMEM)
    plane = arr((4, 128, CIN), BF)
    return call(
        norm_body,
        (plane, plane, arr((2, 8, CIN), F32)),
        (images, gain.reshape(1, CIN), bias.reshape(1, CIN)),
        flops=COST_NORM,
        scratch=(pltpu.VMEM((CIN // LANES, 2, 16, 16, LANES), BF),)
        + (pltpu.VMEM((2, 512, 128), F32),) * (LANES // 128)
        + (pltpu.SemaphoreType.DMA((CIN // LANES,)),),
        specs=[pl.BlockSpec(memory_space=pltpu.HBM), vm, vm],
        out_specs=(vm, vm, vm),
        after=after,
    )


def norm_back_body(*refs):
    xp_ref, own_ref, got_ref, gain_ref, bias_ref, stat_ref, res_own, res_got = refs[:8]
    out_ref, res_ref, mark = refs[8:11]
    bufs = refs[11:]
    core = position()[3]
    for c in range(2):
        res_ref[:, HALF * c : HALF * c + HALF] = jnp.where(core == c, res_own[...], res_got[...])
    mark[...] = jnp.zeros_like(mark)
    for n in range(CIN // LANES):
        lanes = slice(LANES * n, LANES * n + LANES)
        gain, bias = gain_ref[:, lanes], bias_ref[:, lanes]
        mean, rstd = stat_ref[0, :, lanes], stat_ref[1, :, lanes]
        hats, grads, one, two = [], [], [], []
        for i in range(2):
            rows = slice(64 * i, 64 * i + 64)
            m, r = mean[i : i + 1], rstd[i : i + 1]
            h_list, g_list, s1, s2 = [], [], 0.0, 0.0
            for p in range(4):
                hat = (xp_ref[p, rows, lanes].astype(F32) - m) * r
                y = hat * gain + bias
                s = jax.nn.sigmoid(y)
                d = own_ref[p, rows, lanes] + got_ref[p, rows, lanes].astype(F32)
                g = d * (s * (1.0 + y * (1.0 - s))) * gain
                s1 = s1 + jnp.sum(g, axis=0, keepdims=True)
                s2 = s2 + jnp.sum(g * hat, axis=0, keepdims=True)
                h_list.append(hat)
                g_list.append(g)
            hats.append(h_list)
            grads.append(g_list)
            one.append(s1)
            two.append(s2)
        mean1 = group_mean(stack_rows(*one))
        mean2 = group_mean(stack_rows(*two))
        for pj in range(2):
            parts = []
            for i in range(2):
                both = []
                for pi in range(2):
                    p = 2 * pi + pj
                    dx = rstd[i : i + 1] * (
                        grads[i][p] - mean1[i : i + 1] - hats[i][p] * mean2[i : i + 1]
                    )
                    both.append(dx.reshape(8, 1, 8, LANES))
                parts.append(jnp.concatenate(both, axis=1).reshape(128, LANES))
            rows = jnp.concatenate(parts, axis=0)
            for h, buf in enumerate(bufs):
                buf[n % 2, pl.ds(pj, 256, stride=2), :] = rows[:, 128 * h : 128 * h + 128]
        for h, buf in enumerate(bufs):
            at = slice(LANES * n + 128 * h, LANES * n + 128 * h + 128)
            out_ref[:, :, :, at] = buf[n % 2].astype(BF).reshape(2, 16, 16, 128)


def norm_backward(planes, own, got, gain, bias, stat, res_own, res_got):
    vm = pl.BlockSpec(memory_space=pltpu.VMEM)
    return call(
        norm_back_body,
        (arr((2, 16, 16, CIN), BF), arr((128, COUT), BF), arr((8, 128), F32)),
        (planes, own, got, gain.reshape(1, CIN), bias.reshape(1, CIN), stat, res_own, res_got),
        flops=COST_BACK,
        moved=MOVED_BACK,
        scratch=(pltpu.VMEM((2, 512, 128), F32),) * (LANES // 128),
        specs=[vm] * 8,
        out_specs=(vm,) * 3,
        vmem=16,
    )


def shifted(cot, si, sj):
    row = lax.broadcasted_iota(jnp.int32, cot.shape, 0)
    value = cot
    if sj:
        value = jnp.where(row % 8 == 7, 0.0, pltpu.roll(value, cot.shape[0] - 1, 0))
    if si:
        value = jnp.where((row // 8) % 8 == 7, 0.0, pltpu.roll(value, cot.shape[0] - 8, 0))
    return value


def delayed(acc, si, sj):
    row = lax.broadcasted_iota(jnp.int32, acc.shape, 0)
    value = acc
    if sj:
        value = jnp.where(row % 8 == 0, 0.0, pltpu.roll(value, 1, 0))
    if si:
        value = jnp.where((row // 8) % 8 == 0, 0.0, pltpu.roll(value, 8, 0))
    return value


def cot_rows(own_ref, got_ref):
    return jnp.concatenate([own_ref[...], got_ref[...]], axis=0).astype(F32)


def last_tap(z):
    return -(-(z + 1) * 2304 // CIN) - 1


def wgrad_body(act_own, act_got, cot_own, cot_got, *refs):
    ahead, here, behind, far_low, far_high, bias = refs[:6]
    whole, turned, sem = refs[6:9]
    x, _, _, core = position()
    cot = cot_rows(cot_own, cot_got)
    moved = {(si, sj): shifted(cot, si, sj).astype(BF) for si in range(2) for sj in range(2)}
    bias[...] = jnp.broadcast_to(jnp.sum(cot, axis=0, keepdims=True), bias.shape)
    copies = []
    ready = set()
    for t, (ky, kx) in enumerate(TAPS):
        (pi, si), (pj, sj) = source(ky), source(kx)
        p = 2 * pi + pj
        if p not in ready:
            turned[p, :, :128] = act_own[p].T
            turned[p, :, 128:] = act_got[p].T
            ready.add(p)
        grad = jnp.dot(turned[p], moved[si, sj], preferred_element_type=F32).astype(BF)
        for q in range(16):
            n = t * 64 + 4 * q
            r, k = n // PER_CHIP, n % PER_CHIP
            whole[r, k : k + 4] = grad[64 * q : 64 * q + 64].reshape(4, CHUNK, HALF)
        for z in range(4):
            if last_tap(z) != t:
                continue
            far = far_low if z < 2 else far_high
            for d, (out, at) in enumerate(((here, z), (ahead, z), (far, z % 2), (behind, z))):
                copies.append(
                    pltpu.make_async_copy(
                        whole.at[pl.ds(4 * z, 4), pl.ds(QUARTER * turn(x, d, core), QUARTER)],
                        out.at[pl.ds(4 * at, 4)],
                        sem.at[len(copies)],
                    )
                )
                copies[-1].start()
    for copy in copies:
        copy.wait()


def wgrad(act_own, act_got, cot_own, cot_got):
    vm = pl.BlockSpec(memory_space=pltpu.VMEM)
    hbm = pl.BlockSpec(memory_space=pl.ANY)
    full = arr((16, QUARTER, CHUNK, HALF), BF)
    half = arr((8, QUARTER, CHUNK, HALF), BF)
    return call(
        wgrad_body,
        (full, full, full, half, half, arr((8, HALF), F32)),
        (act_own, act_got, cot_own, cot_got),
        flops=COST_WGRAD,
        scratch=(
            pltpu.VMEM((16, PER_CHIP, CHUNK, HALF), BF),
            pltpu.VMEM((4, CIN, 256), BF),
            pltpu.SemaphoreType.DMA((16,)),
        ),
        specs=[vm] * 4,
        out_specs=(hbm,) * 5 + (vm,),
        vmem=24,
    )


def conv_body(*refs):
    here, ahead, behind, far_low, far_high = refs[:5]
    act_own, act_got, cot_own, cot_got, cbias = refs[5:10]
    out_own, out_other, dact_own, dact_other = refs[10:14]
    whole, sem = refs[14], refs[15]
    _, y, _, core = position()
    copies = []
    for z in range(4):
        far = far_low if z < 2 else far_high
        copies.append([])
        for d, part in enumerate((here.at[z], ahead.at[z], far.at[z % 2], behind.at[z])):
            copies[z].append(
                pltpu.make_async_copy(part, whole.at[z, turn(y, d, core)], sem.at[4 * z + d])
            )
    for group in copies:
        for copy in group:
            copy.start()
    cot = cot_rows(cot_own, cot_got)
    moved = {(si, sj): shifted(cot, si, sj).astype(BF) for si in range(2) for sj in range(2)}

    def tap(t):
        rows = []
        for q in range(16):
            n = t * 64 + 4 * q
            r, k = n // PER_CHIP, n % PER_CHIP
            rows.append(whole[r // 4, r % 4, k : k + 4].reshape(64, HALF))
        return jnp.concatenate(rows, axis=0)

    total = jnp.broadcast_to(cbias[...], (256, HALF))
    row = 0
    for t, (ky, kx) in enumerate(TAPS):
        while row < 4 and row * 2304 < (t + 1) * CIN:
            for copy in copies[row]:
                copy.wait()
            row += 1
        (pi, si), (pj, sj) = source(ky), source(kx)
        act = jnp.concatenate([act_own[2 * pi + pj], act_got[2 * pi + pj]], axis=0)
        term = jnp.dot(act, tap(t), preferred_element_type=F32)
        total = total + delayed(term, si, sj)
    result = total.astype(BF)
    out_own[...] = result[:128]
    out_other[...] = result[128:]
    for pi in range(2):
        for pj in range(2):
            acc = None
            for t, (ky, kx) in enumerate(TAPS):
                (a, si), (b, sj) = source(ky), source(kx)
                if (a, b) != (pi, pj):
                    continue
                term = lax.dot_general(
                    moved[si, sj], tap(t), (((1,), (1,)), ((), ())), preferred_element_type=F32
                )
                acc = term if acc is None else acc + term
            dact_own[2 * pi + pj] = acc[:128]
            dact_other[2 * pi + pj] = acc[128:].astype(BF)


def conv(parts, act_own, act_got, cot_own, cot_got, cbias, after):
    vm = pl.BlockSpec(memory_space=pltpu.VMEM)
    hbm = pl.BlockSpec(memory_space=pl.ANY)
    out = arr((128, HALF), BF)
    return call(
        conv_body,
        (out, out, arr((4, 128, CIN), F32), arr((4, 128, CIN), BF)),
        (*parts, act_own, act_got, cot_own, cot_got, cbias),
        flops=COST_CONV,
        moved=MOVED_CONV,
        scratch=(
            pltpu.VMEM((4, 4, PER_CHIP, CHUNK, HALF), BF),
            pltpu.SemaphoreType.DMA((16,)),
        ),
        specs=[hbm] * 5 + [vm] * 5,
        out_specs=(vm,) * 4,
        vmem=32,
        after=after,
    )


def block_body(rows, theirs, out):
    core = position()[3]
    own = jnp.where(core == 0, rows[:, :, :HALF], rows[:, :, HALF:])
    out[pl.ds(18 * core, 18)] = own
    out[pl.ds(18 * (1 - core), 18)] = theirs[...]


def spread_z_body(a0, a2, a1, a3, out):
    _, _, z, core = position()
    for d, ref in enumerate((a0, a1, a2, a3)):
        out[turn(z, d, core)] = ref[...]


def chip_block(kernel, core):
    rows = kernel.reshape(18, CHUNK, COUT)
    theirs = fetch(jnp.where(core == 0, rows[:, :, HALF:], rows[:, :, :HALF]), swap=1)
    return call(block_body, (arr((PER_CHIP, CHUNK, HALF), BF),), (rows, theirs))[0]


def mark_body(out):
    out[...] = jnp.zeros_like(out)


def gather_z(block):
    got = [block] + [fetch(block, dz=2 * d) for d in (2, 1, 3)]
    mark = call(mark_body, (arr((8, 128), F32),), (), flops=COST_MARK, after=(got[2],))[0]
    return mark, call(spread_z_body, (arr((4, PER_CHIP, CHUNK, HALF), BF),), got, flops=COST_SPREAD)[0]


def across_body(ahead, behind, low, high):
    low[...] = ahead[:2]
    high[...] = behind[2:]


def gather_y(level, ahead, behind, after):
    low, high = call(
        across_body,
        (arr((2, PER_CHIP, CHUNK, HALF), BF),) * 2,
        (ahead, behind),
        vmem=12,
        after=after,
    )
    return level, ahead, behind, fetch(low, dy=1), fetch(high, dy=3)


def four(refs, index):
    v = [ref[index].astype(F32) for ref in refs]
    return (v[0] + v[2]) + (v[1] + v[3])


def bias_four(refs, index):
    v = [ref[index].astype(F32) for ref in refs]
    v = [w[0:1] + w[1:2] for w in v]
    return (v[0] + v[2]) + (v[1] + v[3])


def bias_chunk(total):
    high = total.astype(BF).astype(F32)
    row = lax.broadcasted_iota(jnp.int32, (CHUNK, HALF), 0)
    return jnp.where(row == 0, high, jnp.where(row == 1, total - high, 0.0)).astype(BF)


def own_and_sent(shape):
    return (arr(shape, F32),) + (arr(shape, BF),) * 3


def pass_on_body(ahead, behind, low, high, ahead_out, behind_out):
    ahead_out[:8] = (ahead[:8].astype(F32) + low[...].astype(F32)).astype(BF)
    ahead_out[8:] = ahead[8:]
    behind_out[:8] = behind[:8]
    behind_out[8:] = (behind[8:].astype(F32) + high[...].astype(F32)).astype(BF)


def sum_x_body(own, left, right, bias_ref, *outs):
    _, y, _, core = position()
    bias = bias_chunk(bias_ref[0:1])
    for d in range(4):
        there = turn(y, d, core)
        for z in range(4):
            r = 4 * z + there
            total = own[r].astype(F32) + (left[r].astype(F32) + right[r].astype(F32))
            outs[d][QUARTER * z : QUARTER * z + QUARTER] = total.astype(outs[d].dtype)
        outs[d][4 * QUARTER] = bias.astype(outs[d].dtype)


def sum_y_body(*refs):
    ins, outs = refs[:4], refs[4:]
    _, _, z, core = position()
    bias = bias_chunk(bias_four(ins, 4 * QUARTER))
    for d in range(4):
        there = turn(z, d, core)
        total = four(ins, pl.ds(QUARTER * there, QUARTER))
        outs[d][:QUARTER] = total.astype(outs[d].dtype)
        outs[d][QUARTER] = bias.astype(outs[d].dtype)


def sum_z_body(*refs):
    ins, out = refs[:4], refs[4]
    out[:QUARTER] = four(ins, pl.ds(0, QUARTER))
    row = lax.broadcasted_iota(jnp.int32, (CHUNK, HALF), 0)
    out[QUARTER] = jnp.where(row == 0, bias_four(ins, QUARTER), 0.0)


def round_body(part, got, out):
    out[:QUARTER] = ((part[:QUARTER] + got[:QUARTER]) * (1.0 / IMAGES)).astype(BF)
    out[QUARTER] = bias_chunk((part[QUARTER, 0:1] + got[QUARTER, 0:1]) * (1.0 / IMAGES))


def place_body(*refs):
    ins, (mine, theirs, whole) = refs[:4], refs[4:]
    x, _, _, core = position()
    for d, ref in enumerate(ins):
        whole[pl.ds(QUARTER * turn(x, d, core), QUARTER)] = ref[:QUARTER]
    mine[:18] = whole[pl.ds(18 * core, 18)]
    theirs[:18] = whole[pl.ds(18 * (1 - core), 18)]
    bias = bias_chunk(bias_four(ins, QUARTER))
    mine[18] = bias
    theirs[18] = bias


def finish_body(mine, theirs, grad, bias):
    core = position()[3]
    for c in range(2):
        part = jnp.where(core == c, mine[...], theirs[...]).astype(F32)
        grad[:, HALF * c : HALF * c + HALF] = part[:18].reshape(288, HALF)
        bias[:, HALF * c : HALF * c + HALF] = part[18, 0:1] + part[18, 1:2]


def reduce_xy(parts, mark, around):
    ahead, here, behind, far_low, far_high, bias = parts
    low, high = fetch(far_low, dx=3), fetch(far_high, dx=1)
    ahead, behind = call(
        pass_on_body,
        (arr((16, QUARTER, CHUNK, HALF), BF),) * 2,
        (ahead, behind, low, high),
        flops=COST_SUM,
        vmem=16,
        after=(mark,),
    )
    send = call(
        sum_x_body,
        own_and_sent((4 * QUARTER + 1, CHUNK, HALF)),
        (here, fetch(ahead, dx=3), fetch(behind, dx=1), bias),
        flops=COST_SUM,
        vmem=16,
    )
    got = [send[0]] + [fetch(send[4 - d], dy=d) for d in range(1, 4)]
    return call(
        sum_y_body,
        own_and_sent((QUARTER + 1, CHUNK, HALF)),
        got,
        flops=COST_SUM,
        after=around,
    )


def reduce_z(send):
    got = [send[0]] + [fetch(send[4 - d], dz=2 * d) for d in range(1, 4)]
    part = call(sum_z_body, (arr((QUARTER + 1, CHUNK, HALF), F32),), got, flops=COST_SUM)[0]
    return call(
        round_body, (arr((QUARTER + 1, CHUNK, HALF), BF),), (part, pair_low(part))
    )[0]


def spread_x(full, last):
    every = [full] + [fetch(full, dx=d) for d in range(1, 4)]
    mine, theirs = call(
        place_body,
        (arr((19, CHUNK, HALF), BF),) * 2,
        every,
        flops=COST_PLACE,
        scratch=(pltpu.VMEM((PER_CHIP, CHUNK, HALF), BF),),
    )
    grad, bias = call(
        finish_body,
        (arr((288, COUT), F32), arr((1, COUT), F32)),
        (mine, fetch(theirs, swap=1)),
        after=(last,),
    )
    return grad, bias.reshape(COUT)


def local(images, kernel, gn_gain, gn_bias, conv_bias, cotangent):
    core = position()[3]
    cot = cotangent.reshape(128, COUT)
    left, right = cot[:, :HALF], cot[:, HALF:]
    cot_own = jnp.where(core == 0, left, right)
    cot_got = fetch(jnp.where(core == 0, right, left), swap=1)
    block = chip_block(kernel, core)
    act, planes, stat = norm_forward(images, gn_gain, gn_bias, (block,))
    act_got = fetch(act, swap=1)
    grads = wgrad(act, act_got, cot_own, cot_got)
    mark, level = gather_z(block)
    around = fetch(level, dy=1), fetch(level, dy=3)
    send = reduce_xy(grads, mark, around)
    parts = gather_y(level, *around, (send[0],))
    cbias = jnp.where(core == 0, conv_bias[:HALF], conv_bias[HALF:]).reshape(1, HALF)
    full = reduce_z(send)
    out_own, out_other, dact_own, dact_other = conv(
        parts, act, act_got, cot_own, cot_got, cbias, (full,)
    )
    dact_got = fetch(dact_other, swap=1)
    out_got = fetch(out_other, swap=1)
    input_grad, outputs, mark = norm_backward(
        planes, dact_own, dact_got, gn_gain, gn_bias, stat, out_own, out_got
    )
    outputs = outputs.reshape(cotangent.shape)
    kernel_grad, bias_grad = spread_x(full, mark)
    return outputs, input_grad, kernel_grad, bias_grad


def solution(mesh):
    return jax.shard_map(
        local,
        mesh=mesh,
        in_specs=(
            P(AXES, None, None, None),
            P("shard", None),
            P(),
            P(),
            P(),
            P(AXES, None, None, None),
        ),
        out_specs=(
            P(AXES, None, None, None),
            P(AXES, None, None, None),
            P("shard", None),
            P(),
        ),
        check_vma=False,
    )
```

```python
import functools

import jax
import jax.numpy as jnp
from jax import lax
from jax.experimental import pallas as pl
from jax.experimental.pallas import tpu as pltpu
from jax.sharding import PartitionSpec as P

BF = jnp.bfloat16
F32 = jnp.float32
AXES = ("rep", "shard")
CIN, COUT, HALF = 1024, 512, 256
GSIZE = 32
LANES = 256
IMAGES = 512
EPS = 1e-05
MIB = 1024 * 1024
CHUNK, PER_CHIP, QUARTER = 16, 36, 9
COST_NORM, COST_WGRAD, COST_CONV, COST_BACK, COST_SUM, COST_SPREAD, COST_MARK = 10**10, 2 * 10**10, 10**10, 10**9, 10**10, 10**10, 3 * 10**10
MOVED_CONV, MOVED_BACK, COST_PLACE = 0, 0, 2 * 10**10
TAPS = [(ky, kx) for ky in range(3) for kx in range(3)]


def source(k):
    return (0, 0) if k == 1 else (1, 1 if k == 0 else 0)


def position():
    rep, shard = lax.axis_index("rep"), lax.axis_index("shard")
    return lax.rem(rep, 4), lax.rem(shard // 2, 4), shard // 8, lax.rem(shard, 2)


def number(x, y, z, core):
    return ((z % 2) * 4 + x) * 32 + ((z // 2) * 4 + y) * 2 + core


@functools.lru_cache(maxsize=None)
def pairs(dx, dy, dz, swap):
    out = []
    for x in range(4):
        for y in range(4):
            for z in range(8):
                for core in range(2):
                    sign = 1 - 2 * core
                    src = number(
                        (x + sign * dx) % 4, (y + sign * dy) % 4, (z + sign * dz) % 8, core ^ swap
                    )
                    out.append((src, number(x, y, z, core)))
    return sorted(out)


def fetch(value, dx=0, dy=0, dz=0, swap=0):
    with jax.named_scope(f"from_x{dx}_y{dy}_z{dz}_core{swap}"):
        return lax.ppermute(value, AXES, pairs(dx, dy, dz, swap))


def pair_low(value):
    out = []
    for x in range(4):
        for y in range(4):
            for z in range(8):
                for core in range(2):
                    out.append((number(x, y, z ^ 1, core), number(x, y, z, core)))
    with jax.named_scope("from_z_low"):
        return lax.ppermute(value, AXES, sorted(out))


def turn(index, step, core):
    return lax.rem(index + jnp.where(core == 0, step, 4 - step), 4)


def call(body, outs, args, flops=0, moved=None, scratch=(), specs=None, out_specs=None, grid=None, vmem=8, after=(), **kw):
    if after:
        inner, count = body, len(args)
        body = lambda *refs: inner(*refs[:count], *refs[count + len(after) :])
        if specs is None:
            specs = [pl.BlockSpec(memory_space=pltpu.VMEM)] * count
        specs = list(specs) + [pl.BlockSpec(memory_space=pl.ANY)] * len(after)
        args = (*args, *after)
    if moved is None:
        moved = sum(a.size * a.dtype.itemsize for a in (*args[: len(args) - len(after)], *outs))
    params = dict(kw)
    if grid is not None:
        params["grid"] = grid
    if specs is not None:
        params["in_specs"] = specs
    if out_specs is not None:
        params["out_specs"] = out_specs
    return pl.pallas_call(
        body,
        out_shape=outs,
        scratch_shapes=list(scratch),
        compiler_params=pltpu.CompilerParams(vmem_limit_bytes=vmem * MIB),
        cost_estimate=pl.CostEstimate(flops=flops, bytes_accessed=moved, transcendentals=0),
        **params,
    )(*args)


def arr(shape, dtype):
    return jax.ShapeDtypeStruct(shape, dtype)


def group_mean(rows):
    a = lax.broadcasted_iota(jnp.int32, (LANES, LANES), 0) // GSIZE
    b = lax.broadcasted_iota(jnp.int32, (LANES, LANES), 1) // GSIZE
    ones = jnp.where(a == b, 1.0, 0.0).astype(F32)
    total = lax.dot_general(
        rows,
        ones,
        (((1,), (0,)), ((), ())),
        precision=lax.Precision.HIGHEST,
        preferred_element_type=F32,
    )
    return total * (1.0 / (256 * GSIZE))


def stack_rows(a, b):
    row = lax.broadcasted_iota(jnp.int32, (8, LANES), 0)
    return jnp.where(row == 0, a, jnp.where(row == 1, b, 0.0))


def norm_body(x_hbm, gain_ref, bias_ref, act_ref, plane_ref, stat_ref, raw, *rest):
    bufs, sem = rest[:2], rest[2]
    count = CIN // LANES
    copies = [
        pltpu.make_async_copy(
            x_hbm.at[:, :, :, pl.ds(LANES * n, LANES)], raw.at[n], sem.at[n]
        )
        for n in range(count)
    ]
    for copy in copies:
        copy.start()
    for n, copy in enumerate(copies):
        lanes = slice(LANES * n, LANES * n + LANES)
        copy.wait()
        x = raw[n].astype(F32).reshape(2, 256, LANES)
        sums = [jnp.sum(x[i], axis=0, keepdims=True) for i in range(2)]
        mean = group_mean(stack_rows(*sums))
        sq = [jnp.sum(jnp.square(x[i] - mean[i : i + 1]), axis=0, keepdims=True) for i in range(2)]
        rstd = lax.rsqrt(group_mean(stack_rows(*sq)) + EPS)
        stat_ref[0, :, lanes] = mean
        stat_ref[1, :, lanes] = rstd
        for h, buf in enumerate(bufs):
            buf[n % 2] = x[:, :, 128 * h : 128 * h + 128].reshape(512, 128)
        gain, bias = gain_ref[:, lanes], bias_ref[:, lanes]
        for pj in range(2):
            part = jnp.concatenate(
                [buf[n % 2, pl.ds(pj, 256, stride=2), :] for buf in bufs], axis=-1
            )
            part = part.reshape(2, 8, 2, 8, LANES)
            for pi in range(2):
                for i in range(2):
                    xp = part[i, :, pi].reshape(64, LANES)
                    y = (xp - mean[i : i + 1]) * rstd[i : i + 1] * gain + bias
                    rows = slice(64 * i, 64 * i + 64)
                    act_ref[2 * pi + pj, rows, lanes] = (y * jax.nn.sigmoid(y)).astype(BF)
                    plane_ref[2 * pi + pj, rows, lanes] = xp.astype(BF)


def norm_forward(images, gain, bias, after):
    vm = pl.BlockSpec(memory_space=pltpu.VMEM)
    plane = arr((4, 128, CIN), BF)
    return call(
        norm_body,
        (plane, plane, arr((2, 8, CIN), F32)),
        (images, gain.reshape(1, CIN), bias.reshape(1, CIN)),
        flops=COST_NORM,
        scratch=(pltpu.VMEM((CIN // LANES, 2, 16, 16, LANES), BF),)
        + (pltpu.VMEM((2, 512, 128), F32),) * (LANES // 128)
        + (pltpu.SemaphoreType.DMA((CIN // LANES,)),),
        specs=[pl.BlockSpec(memory_space=pltpu.HBM), vm, vm],
        out_specs=(vm, vm, vm),
        after=after,
    )


def norm_prepare_body(xp_ref, gain_ref, bias_ref, stat_ref, hat_ref, slope_ref):
    for n in range(CIN // LANES):
        lanes = slice(LANES * n, LANES * n + LANES)
        gain, bias = gain_ref[:, lanes], bias_ref[:, lanes]
        for i in range(2):
            rows = slice(64 * i, 64 * i + 64)
            m, r = stat_ref[0, i : i + 1, lanes], stat_ref[1, i : i + 1, lanes]
            for p in range(4):
                hat = (xp_ref[p, rows, lanes].astype(F32) - m) * r
                y = hat * gain + bias
                s = jax.nn.sigmoid(y)
                hat_ref[p, rows, lanes] = hat
                slope_ref[p, rows, lanes] = s * (1.0 + y * (1.0 - s)) * gain


def norm_prepare(planes, gain, bias, stat, after):
    return call(
        norm_prepare_body,
        (arr((4, 128, CIN), F32),) * 2,
        (planes, gain.reshape(1, CIN), bias.reshape(1, CIN), stat),
        flops=10**9,
        vmem=12,
        after=after,
    )


def norm_back_body(*refs):
    hat_ref, slope_ref, own_ref, got_ref, stat_ref, res_own, res_got = refs[:7]
    out_ref, res_ref, mark = refs[7:10]
    bufs = refs[10:]
    core = position()[3]
    for c in range(2):
        res_ref[:, HALF * c : HALF * c + HALF] = jnp.where(core == c, res_own[...], res_got[...])
    mark[...] = jnp.zeros_like(mark)
    for n in range(CIN // LANES):
        lanes = slice(LANES * n, LANES * n + LANES)
        rstd = stat_ref[1, :, lanes]
        hats, grads, one, two = [], [], [], []
        for i in range(2):
            rows = slice(64 * i, 64 * i + 64)
            h_list, g_list, s1, s2 = [], [], 0.0, 0.0
            for p in range(4):
                hat = hat_ref[p, rows, lanes]
                d = own_ref[p, rows, lanes] + got_ref[p, rows, lanes].astype(F32)
                g = d * slope_ref[p, rows, lanes]
                s1 = s1 + jnp.sum(g, axis=0, keepdims=True)
                s2 = s2 + jnp.sum(g * hat, axis=0, keepdims=True)
                h_list.append(hat)
                g_list.append(g)
            hats.append(h_list)
            grads.append(g_list)
            one.append(s1)
            two.append(s2)
        mean1 = group_mean(stack_rows(*one))
        mean2 = group_mean(stack_rows(*two))
        for pj in range(2):
            parts = []
            for i in range(2):
                both = []
                for pi in range(2):
                    p = 2 * pi + pj
                    dx = rstd[i : i + 1] * (
                        grads[i][p] - mean1[i : i + 1] - hats[i][p] * mean2[i : i + 1]
                    )
                    both.append(dx.reshape(8, 1, 8, LANES))
                parts.append(jnp.concatenate(both, axis=1).reshape(128, LANES))
            rows = jnp.concatenate(parts, axis=0)
            for h, buf in enumerate(bufs):
                buf[n % 2, pl.ds(pj, 256, stride=2), :] = rows[:, 128 * h : 128 * h + 128]
        for h, buf in enumerate(bufs):
            at = slice(LANES * n + 128 * h, LANES * n + 128 * h + 128)
            out_ref[:, :, :, at] = buf[n % 2].astype(BF).reshape(2, 16, 16, 128)


def norm_backward(hat, slope, own, got, stat, res_own, res_got):
    vm = pl.BlockSpec(memory_space=pltpu.VMEM)
    return call(
        norm_back_body,
        (arr((2, 16, 16, CIN), BF), arr((128, COUT), BF), arr((8, 128), F32)),
        (hat, slope, own, got, stat, res_own, res_got),
        flops=COST_BACK,
        moved=MOVED_BACK,
        scratch=(pltpu.VMEM((2, 512, 128), F32),) * (LANES // 128),
        specs=[vm] * 7,
        out_specs=(vm,) * 3,
        vmem=16,
    )


def shifted(cot, si, sj):
    row = lax.broadcasted_iota(jnp.int32, cot.shape, 0)
    value = cot
    if sj:
        value = jnp.where(row % 8 == 7, 0.0, pltpu.roll(value, cot.shape[0] - 1, 0))
    if si:
        value = jnp.where((row // 8) % 8 == 7, 0.0, pltpu.roll(value, cot.shape[0] - 8, 0))
    return value


def delayed(acc, si, sj):
    row = lax.broadcasted_iota(jnp.int32, acc.shape, 0)
    value = acc
    if sj:
        value = jnp.where(row % 8 == 0, 0.0, pltpu.roll(value, 1, 0))
    if si:
        value = jnp.where((row // 8) % 8 == 0, 0.0, pltpu.roll(value, 8, 0))
    return value


def cot_rows(own_ref, got_ref):
    return jnp.concatenate([own_ref[...], got_ref[...]], axis=0).astype(F32)


def last_tap(z):
    return -(-(z + 1) * 2304 // CIN) - 1


def wgrad_body(act_own, act_got, cot_own, cot_got, *refs):
    ahead, here, behind, far_low, far_high, bias = refs[:6]
    whole, turned, sem = refs[6:9]
    x, _, _, core = position()
    cot = cot_rows(cot_own, cot_got)
    moved = {(si, sj): shifted(cot, si, sj).astype(BF) for si in range(2) for sj in range(2)}
    bias[...] = jnp.broadcast_to(jnp.sum(cot, axis=0, keepdims=True), bias.shape)
    copies = []
    ready = set()
    for t, (ky, kx) in enumerate(TAPS):
        (pi, si), (pj, sj) = source(ky), source(kx)
        p = 2 * pi + pj
        if p not in ready:
            turned[p, :, :128] = act_own[p].T
            turned[p, :, 128:] = act_got[p].T
            ready.add(p)
        grad = jnp.dot(turned[p], moved[si, sj], preferred_element_type=F32).astype(BF)
        for q in range(16):
            n = t * 64 + 4 * q
            r, k = n // PER_CHIP, n % PER_CHIP
            whole[r, k : k + 4] = grad[64 * q : 64 * q + 64].reshape(4, CHUNK, HALF)
        for z in range(4):
            if last_tap(z) != t:
                continue
            far = far_low if z < 2 else far_high
            for d, (out, at) in enumerate(((here, z), (ahead, z), (far, z % 2), (behind, z))):
                copies.append(
                    pltpu.make_async_copy(
                        whole.at[pl.ds(4 * z, 4), pl.ds(QUARTER * turn(x, d, core), QUARTER)],
                        out.at[pl.ds(4 * at, 4)],
                        sem.at[len(copies)],
                    )
                )
                copies[-1].start()
    for copy in copies:
        copy.wait()


def wgrad(act_own, act_got, cot_own, cot_got):
    vm = pl.BlockSpec(memory_space=pltpu.VMEM)
    hbm = pl.BlockSpec(memory_space=pl.ANY)
    full = arr((16, QUARTER, CHUNK, HALF), BF)
    half = arr((8, QUARTER, CHUNK, HALF), BF)
    return call(
        wgrad_body,
        (full, full, full, half, half, arr((8, HALF), F32)),
        (act_own, act_got, cot_own, cot_got),
        flops=COST_WGRAD,
        scratch=(
            pltpu.VMEM((16, PER_CHIP, CHUNK, HALF), BF),
            pltpu.VMEM((4, CIN, 256), BF),
            pltpu.SemaphoreType.DMA((16,)),
        ),
        specs=[vm] * 4,
        out_specs=(hbm,) * 5 + (vm,),
        vmem=24,
    )


def conv_body(*refs):
    here, ahead, behind, far_low, far_high = refs[:5]
    act_own, act_got, cot_own, cot_got, cbias = refs[5:10]
    out_own, out_other, dact_own, dact_other = refs[10:14]
    whole, sem = refs[14], refs[15]
    _, y, _, core = position()
    copies = []
    for z in range(4):
        far = far_low if z < 2 else far_high
        copies.append([])
        for d, part in enumerate((here.at[z], ahead.at[z], far.at[z % 2], behind.at[z])):
            copies[z].append(
                pltpu.make_async_copy(part, whole.at[z, turn(y, d, core)], sem.at[4 * z + d])
            )
    for group in copies:
        for copy in group:
            copy.start()
    cot = cot_rows(cot_own, cot_got)
    moved = {(si, sj): shifted(cot, si, sj).astype(BF) for si in range(2) for sj in range(2)}

    def tap(t):
        rows = []
        for q in range(16):
            n = t * 64 + 4 * q
            r, k = n // PER_CHIP, n % PER_CHIP
            rows.append(whole[r // 4, r % 4, k : k + 4].reshape(64, HALF))
        return jnp.concatenate(rows, axis=0)

    total = jnp.broadcast_to(cbias[...], (256, HALF))
    row = 0
    for t, (ky, kx) in enumerate(TAPS):
        while row < 4 and row * 2304 < (t + 1) * CIN:
            for copy in copies[row]:
                copy.wait()
            row += 1
        (pi, si), (pj, sj) = source(ky), source(kx)
        act = jnp.concatenate([act_own[2 * pi + pj], act_got[2 * pi + pj]], axis=0)
        term = jnp.dot(act, tap(t), preferred_element_type=F32)
        total = total + delayed(term, si, sj)
    result = total.astype(BF)
    out_own[...] = result[:128]
    out_other[...] = result[128:]
    for pi in range(2):
        for pj in range(2):
            acc = None
            for t, (ky, kx) in enumerate(TAPS):
                (a, si), (b, sj) = source(ky), source(kx)
                if (a, b) != (pi, pj):
                    continue
                term = lax.dot_general(
                    moved[si, sj], tap(t), (((1,), (1,)), ((), ())), preferred_element_type=F32
                )
                acc = term if acc is None else acc + term
            dact_own[2 * pi + pj] = acc[:128]
            dact_other[2 * pi + pj] = acc[128:].astype(BF)


def conv(parts, act_own, act_got, cot_own, cot_got, cbias, after):
    vm = pl.BlockSpec(memory_space=pltpu.VMEM)
    hbm = pl.BlockSpec(memory_space=pl.ANY)
    out = arr((128, HALF), BF)
    return call(
        conv_body,
        (out, out, arr((4, 128, CIN), F32), arr((4, 128, CIN), BF)),
        (*parts, act_own, act_got, cot_own, cot_got, cbias),
        flops=COST_CONV,
        moved=MOVED_CONV,
        scratch=(
            pltpu.VMEM((4, 4, PER_CHIP, CHUNK, HALF), BF),
            pltpu.SemaphoreType.DMA((16,)),
        ),
        specs=[hbm] * 5 + [vm] * 5,
        out_specs=(vm,) * 4,
        vmem=32,
        after=after,
    )


def block_body(rows, theirs, out):
    core = position()[3]
    own = jnp.where(core == 0, rows[:, :, :HALF], rows[:, :, HALF:])
    out[pl.ds(18 * core, 18)] = own
    out[pl.ds(18 * (1 - core), 18)] = theirs[...]


def spread_z_body(a0, a2, a1, a3, out):
    _, _, z, core = position()
    for d, ref in enumerate((a0, a1, a2, a3)):
        out[turn(z, d, core)] = ref[...]


def chip_block(kernel, core):
    rows = kernel.reshape(18, CHUNK, COUT)
    theirs = fetch(jnp.where(core == 0, rows[:, :, HALF:], rows[:, :, :HALF]), swap=1)
    return call(block_body, (arr((PER_CHIP, CHUNK, HALF), BF),), (rows, theirs))[0]


def mark_body(out):
    out[...] = jnp.zeros_like(out)


def gather_z(block):
    got = [block] + [fetch(block, dz=2 * d) for d in (2, 1, 3)]
    mark = call(mark_body, (arr((8, 128), F32),), (), flops=COST_MARK, after=(got[2],))[0]
    return mark, call(spread_z_body, (arr((4, PER_CHIP, CHUNK, HALF), BF),), got, flops=COST_SPREAD)[0]


def across_body(ahead, behind, low, high):
    low[...] = ahead[:2]
    high[...] = behind[2:]


def gather_y(level, ahead, behind, after):
    low, high = call(
        across_body,
        (arr((2, PER_CHIP, CHUNK, HALF), BF),) * 2,
        (ahead, behind),
        vmem=12,
        after=after,
    )
    return level, ahead, behind, fetch(low, dy=1), fetch(high, dy=3)


def four(refs, index):
    v = [ref[index].astype(F32) for ref in refs]
    return (v[0] + v[2]) + (v[1] + v[3])


def bias_four(refs, index):
    v = [ref[index].astype(F32) for ref in refs]
    v = [w[0:1] + w[1:2] for w in v]
    return (v[0] + v[2]) + (v[1] + v[3])


def bias_chunk(total):
    high = total.astype(BF).astype(F32)
    row = lax.broadcasted_iota(jnp.int32, (CHUNK, HALF), 0)
    return jnp.where(row == 0, high, jnp.where(row == 1, total - high, 0.0)).astype(BF)


def own_and_sent(shape):
    return (arr(shape, F32),) + (arr(shape, BF),) * 3


def pass_on_body(ahead, behind, low, high, ahead_out, behind_out):
    ahead_out[:8] = (ahead[:8].astype(F32) + low[...].astype(F32)).astype(BF)
    ahead_out[8:] = ahead[8:]
    behind_out[:8] = behind[:8]
    behind_out[8:] = (behind[8:].astype(F32) + high[...].astype(F32)).astype(BF)


def sum_x_body(own, left, right, bias_ref, *outs):
    _, y, _, core = position()
    bias = bias_chunk(bias_ref[0:1])
    for d in range(4):
        there = turn(y, d, core)
        for z in range(4):
            r = 4 * z + there
            total = own[r].astype(F32) + (left[r].astype(F32) + right[r].astype(F32))
            outs[d][QUARTER * z : QUARTER * z + QUARTER] = total.astype(outs[d].dtype)
        outs[d][4 * QUARTER] = bias.astype(outs[d].dtype)


def sum_y_body(*refs):
    ins, outs = refs[:4], refs[4:]
    _, _, z, core = position()
    bias = bias_chunk(bias_four(ins, 4 * QUARTER))
    for d in range(4):
        there = turn(z, d, core)
        total = four(ins, pl.ds(QUARTER * there, QUARTER))
        outs[d][:QUARTER] = total.astype(outs[d].dtype)
        outs[d][QUARTER] = bias.astype(outs[d].dtype)


def sum_z_body(*refs):
    ins, out = refs[:4], refs[4]
    out[:QUARTER] = four(ins, pl.ds(0, QUARTER))
    row = lax.broadcasted_iota(jnp.int32, (CHUNK, HALF), 0)
    out[QUARTER] = jnp.where(row == 0, bias_four(ins, QUARTER), 0.0)


def round_body(part, got, out):
    out[:QUARTER] = ((part[:QUARTER] + got[:QUARTER]) * (1.0 / IMAGES)).astype(BF)
    out[QUARTER] = bias_chunk((part[QUARTER, 0:1] + got[QUARTER, 0:1]) * (1.0 / IMAGES))


def place_body(*refs):
    ins, (mine, theirs, whole) = refs[:4], refs[4:]
    x, _, _, core = position()
    for d, ref in enumerate(ins):
        whole[pl.ds(QUARTER * turn(x, d, core), QUARTER)] = ref[:QUARTER]
    mine[:18] = whole[pl.ds(18 * core, 18)]
    theirs[:18] = whole[pl.ds(18 * (1 - core), 18)]
    bias = bias_chunk(bias_four(ins, QUARTER))
    mine[18] = bias
    theirs[18] = bias


def finish_body(mine, theirs, grad, bias):
    core = position()[3]
    for c in range(2):
        part = jnp.where(core == c, mine[...], theirs[...]).astype(F32)
        grad[:, HALF * c : HALF * c + HALF] = part[:18].reshape(288, HALF)
        bias[:, HALF * c : HALF * c + HALF] = part[18, 0:1] + part[18, 1:2]


def reduce_xy(parts, mark, around, ready):
    ahead, here, behind, far_low, far_high, bias = parts
    low, high = fetch(far_low, dx=3), fetch(far_high, dx=1)
    ahead, behind = call(
        pass_on_body,
        (arr((16, QUARTER, CHUNK, HALF), BF),) * 2,
        (ahead, behind, low, high),
        flops=COST_SUM,
        vmem=16,
        after=(mark,),
    )
    send = call(
        sum_x_body,
        own_and_sent((4 * QUARTER + 1, CHUNK, HALF)),
        (here, fetch(ahead, dx=3), fetch(behind, dx=1), bias),
        flops=COST_SUM,
        vmem=16,
        after=ready,
    )
    got = [send[0]] + [fetch(send[4 - d], dy=d) for d in range(1, 4)]
    return call(
        sum_y_body,
        own_and_sent((QUARTER + 1, CHUNK, HALF)),
        got,
        flops=COST_SUM,
        after=around,
    )


def reduce_z(send):
    got = [send[0]] + [fetch(send[4 - d], dz=2 * d) for d in range(1, 4)]
    part = call(sum_z_body, (arr((QUARTER + 1, CHUNK, HALF), F32),), got, flops=COST_SUM)[0]
    return call(
        round_body, (arr((QUARTER + 1, CHUNK, HALF), BF),), (part, pair_low(part))
    )[0]


def spread_x(full, last):
    every = [full] + [fetch(full, dx=d) for d in range(1, 4)]
    mine, theirs = call(
        place_body,
        (arr((19, CHUNK, HALF), BF),) * 2,
        every,
        flops=COST_PLACE,
        scratch=(pltpu.VMEM((PER_CHIP, CHUNK, HALF), BF),),
    )
    grad, bias = call(
        finish_body,
        (arr((288, COUT), F32), arr((1, COUT), F32)),
        (mine, fetch(theirs, swap=1)),
        after=(last,),
    )
    return grad, bias.reshape(COUT)


def local(images, kernel, gn_gain, gn_bias, conv_bias, cotangent):
    core = position()[3]
    cot = cotangent.reshape(128, COUT)
    left, right = cot[:, :HALF], cot[:, HALF:]
    cot_own = jnp.where(core == 0, left, right)
    cot_got = fetch(jnp.where(core == 0, right, left), swap=1)
    block = chip_block(kernel, core)
    act, planes, stat = norm_forward(images, gn_gain, gn_bias, (block,))
    act_got = fetch(act, swap=1)
    grads = wgrad(act, act_got, cot_own, cot_got)
    mark, level = gather_z(block)
    around = fetch(level, dy=1), fetch(level, dy=3)
    hat, slope = norm_prepare(planes, gn_gain, gn_bias, stat, (level,))
    send = reduce_xy(grads, mark, around, (slope,))
    parts = gather_y(level, *around, (send[0],))
    cbias = jnp.where(core == 0, conv_bias[:HALF], conv_bias[HALF:]).reshape(1, HALF)
    full = reduce_z(send)
    out_own, out_other, dact_own, dact_other = conv(
        parts, act, act_got, cot_own, cot_got, cbias, (full,)
    )
    dact_got = fetch(dact_other, swap=1)
    out_got = fetch(out_other, swap=1)
    input_grad, outputs, mark = norm_backward(
        hat, slope, dact_own, dact_got, stat, out_own, out_got
    )
    outputs = outputs.reshape(cotangent.shape)
    kernel_grad, bias_grad = spread_x(full, mark)
    return outputs, input_grad, kernel_grad, bias_grad


def solution(mesh):
    return jax.shard_map(
        local,
        mesh=mesh,
        in_specs=(
            P(AXES, None, None, None),
            P("shard", None),
            P(),
            P(),
            P(),
            P(AXES, None, None, None),
        ),
        out_specs=(
            P(AXES, None, None, None),
            P(AXES, None, None, None),
            P("shard", None),
            P(),
        ),
        check_vma=False,
    )
```
